256 devices in a mesh: aux: 8 (over y, core), tile: 32 (over z, x).
Axes of the slice: x: 4, y: 4, z: 8, core: 2. Of those that a mesh axis runs over, the one named last changes fastest.
Arguments:
- integrals: bfloat16 [32, 4, 128, 32, 128], P('tile', None, None, 'aux'), may hold values from -6 to 6
- orbitals: bfloat16 [4096, 1024], P('tile'), may hold values from -0.25 to 0.25
- pair_tiles: int32 [32, 4], replicated, may hold values from 0 to 31, as said below
- pair_live: int32 [32, 4], replicated, may hold values from 0 to 1, as said below
- occ_live: int32 [32, 8], replicated, may hold values from 0 to 1, as said below
Outputs:
- exchange_blocks: float32 [32, 4, 128, 128], P('tile', None, 'aux')
The draws below stay inside these ranges and needn't reach their ends.
Inputs may be any that keep to these rules, and one draw needn't show every extreme that they name: `pair_tiles`: row t holds 4 distinct tiles, none equal to t. `pair_live`: in each row the live slots come first; each tile has 1 to 4 live slots, and some tile has all 4. `occ_live`: each row has exactly 4 ones.
All inputs are finite; a program needn't handle non-finite values.
Results may differ from the reference program's by a relative error of at most 0.0038.
Values may be sent and summed in bfloat16 or wider, within the bound.
No kernel may reach another device: no remote copies, remote signals or barrier semaphores. Data moves between devices by JAX's collectives and lax.ppermute only.
A program may use at most 64 MiB of HBM per device.

```python
import math
import jax
import jax.numpy as jnp
from jax import lax

TS = 128
NOCC = 1024
SLOTS = 4
OCC_LIVE = 4
Q_DEV = 4
NAUX = 32
NT = 32
NBF = 4096
N_AUX = 8


def draw_pair_tiles(key, part):
    key = jax.random.fold_in(key, 11)
    tile_key, pick_key = jax.random.split(key)
    tile_keys = jax.random.split(tile_key, NT)
    orders = jax.vmap(lambda single: jax.random.permutation(single, NT - 1))(tile_keys)
    picks = jax.random.permutation(pick_key, NT)[:3]
    rows = jnp.arange(NT)
    desired = jnp.where(rows == picks[0], NT - 2, jnp.where(rows == picks[1], NT // 2 - 1, jnp.where(rows == picks[2], 0, orders[:, 0])))
    swapped = jnp.where(orders == desired[:, None], orders[:, :1], orders)
    swapped = swapped.at[:, 0].set(desired)
    offsets = swapped[:, :SLOTS]
    return ((rows[:, None] + 1 + offsets) % NT).astype(jnp.int32)


def draw_pair_live(key, part):
    key = jax.random.fold_in(key, 12)
    count_key, pick_key = jax.random.split(key)
    counts = jax.random.randint(count_key, (NT,), 1, SLOTS + 1)
    full_tile = jax.random.randint(pick_key, (), 0, NT)
    counts = jnp.where(jnp.arange(NT) == full_tile, SLOTS, counts)
    return (jnp.arange(SLOTS)[None, :] < counts[:, None]).astype(jnp.int32)


def draw_occ_live(key, part):
    key = jax.random.fold_in(key, 13)
    tile_keys = jax.random.split(key, NT)
    orders = jax.vmap(lambda single: jax.random.permutation(single, NOCC // TS))(tile_keys)
    chosen = orders[:, :OCC_LIVE]
    return jnp.any(chosen[:, :, None] == jnp.arange(NOCC // TS)[None, None, :], axis=1).astype(jnp.int32)


def shard_levels(own_key, shape, cuts, least, high):
    gain, own = 1.0, jax.random.fold_in(own_key, 6)
    for position, blocks in cuts:
        heights = jnp.exp(jax.random.uniform(jax.random.fold_in(own, position), (blocks,), jnp.float32, least / len(cuts), high / len(cuts)))
        gain = gain * jnp.repeat(heights, shape[position] // blocks).reshape([-1 if axis == position else 1 for axis in range(len(shape))])
    return gain


def centred(stream_key, shape, scale, bound, pieces=(), kind=jnp.bfloat16):
    array = jax.random.normal(stream_key, shape, jnp.float32) * scale
    if len(pieces) > 0:
        array = shard_levels(stream_key, shape, pieces, -0.22, 0.18) * array
    return jnp.clip(array, min=-bound, max=bound).astype(kind)


def setup_inputs(seed: int = 0) -> dict:
    key_of = jax.random.split(jax.random.key(seed), 6)
    integrals = centred(key_of[0], (NT, SLOTS, TS, NAUX, TS), 1.0, 6.0, ((0, 32), (3, 8)))
    orbitals = centred(key_of[1], (NBF, NOCC), (TS * SLOTS) ** -0.5, 0.25, ((0, 32),))
    pair_tiles = draw_pair_tiles(jax.random.fold_in(key_of[5], 71), 0)
    pair_live = draw_pair_live(jax.random.fold_in(key_of[5], 71), 0)
    occ_live = draw_occ_live(jax.random.fold_in(key_of[5], 71), 0)
    return {"integrals": integrals, "orbitals": orbitals, "pair_tiles": pair_tiles, "pair_live": pair_live, "occ_live": occ_live}


def reference(integrals, orbitals, pair_tiles, pair_live, occ_live):
    full_mask = jnp.repeat(jnp.repeat(occ_live, TS, axis=1), TS, axis=0)
    masked = orbitals * full_mask.astype(orbitals.dtype)
    partners = masked.reshape(NT, TS, NOCC)[pair_tiles]
    slot_live = pair_live.astype(jnp.float32)
    norm_scale = 1.0 / math.sqrt(NAUX * NOCC)

    def aux_group(totals, index):
        eri_block = lax.dynamic_slice_in_dim(integrals, index * Q_DEV, Q_DEV, 3).astype(jnp.float32)

        def occ_step(inner_sum, occ_index):
            occ_coeffs = lax.dynamic_slice_in_dim(partners, occ_index * TS, TS, 3).astype(jnp.float32)
            occ_coeffs = occ_coeffs * slot_live[:, :, None, None]
            half_field = jnp.einsum('msbi,msbqa->miqa', occ_coeffs, eri_block)
            half_field = lax.optimization_barrier(half_field.astype(jnp.bfloat16)).astype(jnp.float32)
            gram_terms = [jnp.einsum('miqa,miqb->mab', half_field, half_field[pair_tiles[:, slot]]) for slot in range(SLOTS)]
            return (inner_sum + jnp.stack(gram_terms, axis=1), None)
        totals, _ = lax.scan(occ_step, totals, jnp.arange(NOCC // TS, dtype=jnp.int32))
        return (totals, None)
    totals, _ = lax.scan(aux_group, jnp.zeros((NT, SLOTS, TS, TS), jnp.float32), jnp.arange(N_AUX, dtype=jnp.int32))
    return totals * norm_scale * slot_live[:, :, None, None]
```

```python
import functools
import math

import jax
import jax.numpy as jnp
from jax import lax
from jax.experimental import pallas as pl
from jax.experimental.pallas import tpu as pltpu
from jax.sharding import Mesh, PartitionSpec as P

NY, NC, NZ, NX = 4, 2, 8, 4
TILES, SLOTS, TS = 32, 4, 128
OCC, LIVE = 8, 4
AUXROWS = 4
HALF = TS // 2
ROWS = TS // (NY * NC)
SCALE = 1.0 / math.sqrt(32768.0)
BF = jnp.bfloat16
F32 = jnp.float32
VMEM = pl.BlockSpec(memory_space=pltpu.VMEM)
SMEM = pl.BlockSpec(memory_space=pltpu.SMEM)


def prep_kernel(pos, occ_live, eri, orb, chunks, coeffs, split):
    core, z, tile = pos[1], pos[2], pos[2] * NX + pos[3]
    row = lax.broadcasted_iota(jnp.int32, (TS, TS), 0)
    col = lax.broadcasted_iota(jnp.int32, (TS, TS), 1)
    block_nu = TS // AUXROWS
    perm = (col == (row % block_nu) * AUXROWS + row // block_nu).astype(BF)
    for slot in range(SLOTS):
        for part in range(AUXROWS):
            start = (slot * AUXROWS + part) * TS
            mixed = jnp.dot(perm, eri[pl.ds(start, TS), :], preferred_element_type=F32).astype(BF)
            for aux in range(AUXROWS):
                split[aux, slot, pl.ds(part * block_nu, block_nu), :] = mixed[aux * block_nu:(aux + 1) * block_nu]
    for step in range(NZ):
        target = (z + step) % NZ
        hop = jnp.where(core == target // 4, 0, 1)
        for j in range(2):
            chunks[step, j] = split[target % 4, hop * 2 + j]
    count = jnp.int32(0)
    for occ in range(OCC):
        live = occ_live[tile, occ]

        @pl.when(live != 0)
        def _():
            flipped = orb[:, occ * TS:(occ + 1) * TS].astype(F32).T.astype(BF)
            coeffs[count] = jnp.where(core == 0, flipped[:HALF], flipped[HALF:])

        count = count + jnp.where(live != 0, 1, 0)


def prep(pos, occ_live, eri, orb):
    return pl.pallas_call(
        prep_kernel,
        out_shape=(
            jax.ShapeDtypeStruct((NZ, 2, TS, TS), BF),
            jax.ShapeDtypeStruct((LIVE, HALF, TS), BF),
        ),
        in_specs=[SMEM, SMEM, VMEM, VMEM],
        out_specs=(VMEM, VMEM),
        scratch_shapes=[pltpu.VMEM((AUXROWS, SLOTS, TS, TS), BF)],
        compiler_params=pltpu.CompilerParams(vmem_limit_bytes=16 * 2**20),
        name="prep",
    )(pos, occ_live, eri, orb)


def main_kernel(pos, pair_tiles, pair_live, occ_live,
                own0, own_r, own_l, own_r2, own_l2,
                oth0, oth_r, oth_l, oth_r2, oth_l2,
                c0, cr1, cl1, cr2, cl2, cr3, cl3, cr4, cl4,
                keep, send, dense, field, block):
    core, z, x = pos[1], pos[2], pos[3]

    def place(piece, zp, lo, hi):
        def body(entry, carry):
            tile = zp * NX + (x - entry) % NX
            count = jnp.int32(0)
            for occ in range(OCC):
                live = occ_live[tile, occ] != 0
                data = piece[entry - lo, jnp.minimum(count, LIVE - 1)]
                dense[tile, pl.ds(occ * HALF, HALF), :] = jnp.where(live, data, jnp.zeros_like(data))
                count = count + jnp.where(live, 1, 0)
            return carry

        lax.fori_loop(lo, hi, body, 0)

    for piece, shift, lo, hi in (
        (c0, 0, 0, 4), (cr1, -1, 0, 4), (cl1, 1, 0, 4), (cr2, -2, 0, 4), (cl2, 2, 0, 4),
        (cr3, -3, 0, 4), (cl3, 3, 0, 4), (cr4, 4, 0, 2), (cl4, 4, 2, 4),
    ):
        place(piece, (z + shift) % NZ, lo, hi)

    def transform(xp, own, oth, lo, hi, own_lo, oth_lo):
        def body(step, carry):
            zp = (z - step - 4 * core) % NZ
            tile = zp * NX + xp
            coeffs, eris = [], []
            for part, ref, index in (
                (core, own, step - own_lo),
                (1 - core, oth, (step + 4) % NZ - oth_lo),
            ):
                for j in range(2):
                    slot = part * 2 + j
                    live = pair_live[tile, slot] != 0
                    eri = ref[index, j]
                    eris.append(jnp.where(live, eri, jnp.zeros_like(eri)))
                    coeffs.append(dense[pair_tiles[tile, slot]])
            half = jnp.dot(
                jnp.concatenate(coeffs, axis=1), jnp.concatenate(eris, axis=0), preferred_element_type=F32
            )
            field[tile] = half.astype(BF)
            return carry

        lax.fori_loop(lo, hi, body, 0)

    transform(x, own0, oth0, 0, 8, 0, 0)
    transform((x - 1) % NX, own_r, oth_r, 0, 8, 0, 0)
    transform((x + 1) % NX, own_l, oth_l, 0, 8, 0, 0)
    transform((x + 2) % NX, own_r2, oth_l2, 0, 4, 0, 4)
    transform((x + 2) % NX, own_l2, oth_r2, 4, 8, 4, 0)

    def gram(zp, carry):
        tile = zp * NX + x
        partners = jnp.concatenate([field[pair_tiles[tile, slot]] for slot in range(SLOTS)], axis=1)
        block[...] = lax.dot_general(
            field[tile], partners, (((0,), (0,)), ((), ())), preferred_element_type=F32
        )
        for y in range(NY):
            near = pl.multiple_of(y * 2 * ROWS + core * ROWS, ROWS)
            far = pl.multiple_of(y * 2 * ROWS + (1 - core) * ROWS, ROWS)
            for slot in range(SLOTS):
                keep[y, zp, slot] = block[pl.ds(near, ROWS), slot * TS:(slot + 1) * TS]
                send[y, zp, slot] = block[pl.ds(far, ROWS), slot * TS:(slot + 1) * TS]
        return carry

    lax.fori_loop(0, NZ, gram, 0)


def exchange(*operands):
    shape = jax.ShapeDtypeStruct((NY, NZ, SLOTS, ROWS, TS), F32)
    return pl.pallas_call(
        main_kernel,
        out_shape=(shape, shape),
        in_specs=[SMEM] * 4 + [VMEM] * (len(operands) - 4),
        out_specs=(VMEM, VMEM),
        scratch_shapes=[
            pltpu.VMEM((TILES, OCC * HALF, TS), BF),
            pltpu.VMEM((TILES, OCC * HALF, TS), BF),
            pltpu.VMEM((TS, SLOTS * TS), F32),
        ],
        compiler_params=pltpu.CompilerParams(vmem_limit_bytes=40 * 2**20),
        name="exchange",
    )(*operands)


def shift(value, axis, size, by):
    return lax.ppermute(value, axis, [(i, (i + by) % size) for i in range(size)])


def spread(value, step):
    pairs = []
    for z in range(NZ):
        target = (z + step) % NZ
        core = target // 4
        pairs.append((core * NZ + z, target))
        pairs.append(((1 - core) * NZ + z, NZ + (target + 4) % NZ))
    return lax.ppermute(value, ("c", "z"), pairs)


def swap(value):
    return lax.ppermute(value, "c", [(0, 1), (1, 0)])


def shards(integrals, orbitals, pair_tiles, pair_live, occ_live):
    pos = jnp.stack([lax.axis_index(name).astype(jnp.int32) for name in ("y", "c", "z", "x")])
    tile = pos[2] * NX + pos[3]
    eri = integrals.reshape(SLOTS * TS * AUXROWS, TS)
    chunks, coeffs = prep(pos, occ_live, eri, orbitals)

    own0 = jnp.stack([spread(chunks[step], step) for step in range(NZ)])
    c0 = jnp.stack([coeffs] + [shift(coeffs, "x", NX, by) for by in (1, 2, 3)])

    own_r, own_l = shift(own0, "x", NX, 1), shift(own0, "x", NX, -1)
    cr1, cl1 = shift(c0, "z", NZ, 1), shift(c0, "z", NZ, -1)
    oth0 = swap(own0)
    own_r2, own_l2 = shift(own_r[:4], "x", NX, 1), shift(own_l[4:], "x", NX, -1)
    cr2, cl2 = shift(cr1, "z", NZ, 1), shift(cl1, "z", NZ, -1)
    oth_r, oth_l = swap(own_r), swap(own_l)
    cr3, cl3 = shift(cr2, "z", NZ, 1), shift(cl2, "z", NZ, -1)
    oth_r2, oth_l2 = swap(own_r2), swap(own_l2)
    cr4, cl4 = shift(cr3[:2], "z", NZ, 1), shift(cl3[2:], "z", NZ, -1)

    keep, send = exchange(
        pos, pair_tiles, pair_live, occ_live,
        own0, own_r, own_l, own_r2, own_l2, oth0, oth_r, oth_l, oth_r2, oth_l2,
        c0, cr1, cl1, cr2, cl2, cr3, cl3, cr4, cl4,
    )
    partial = (keep + swap(send)).reshape(NY * NZ, SLOTS, ROWS, TS)
    parts = lax.all_to_all(partial, ("y", "z"), split_axis=0, concat_axis=0, tiled=True)
    flags = lax.dynamic_index_in_dim(pair_live, tile, 0, keepdims=False).astype(F32) * SCALE
    return (jnp.sum(parts, axis=0) * flags[:, None, None])[None]


def solution(mesh):
    grid = Mesh(mesh.devices.reshape(NY, NC, NZ, NX), ("y", "c", "z", "x"))
    return jax.shard_map(
        shards,
        mesh=grid,
        in_specs=(
            P(("z", "x"), None, None, ("y", "c"), None),
            P(("z", "x"), None),
            P(),
            P(),
            P(),
        ),
        out_specs=P(("z", "x"), None, ("y", "c"), None),
        check_vma=False,
    )
```

```python
import functools
import math

import jax
import jax.numpy as jnp
from jax import lax
from jax.experimental import pallas as pl
from jax.experimental.pallas import tpu as pltpu
from jax.sharding import Mesh, PartitionSpec as P

NY, NC, NZ, NX = 4, 2, 8, 4
TILES, SLOTS, TS = 32, 4, 128
OCC, LIVE = 8, 4
AUXROWS = 4
HALF = TS // 2
ROWS = TS // (NY * NC)
SCALE = 1.0 / math.sqrt(32768.0)
BF = jnp.bfloat16
F32 = jnp.float32
VMEM = pl.BlockSpec(memory_space=pltpu.VMEM)
SMEM = pl.BlockSpec(memory_space=pltpu.SMEM)
ANY = pl.BlockSpec(memory_space=pl.ANY)


def prep_kernel(pos, occ_live, eri, orb, keep, give, coeffs, rows, cols, sems):
    core, tile = pos[1], pos[2] * NX + pos[3]
    load_cols = pltpu.make_async_copy(orb, cols, sems.at[0])
    load_rows = pltpu.make_async_copy(eri, rows, sems.at[1])
    load_cols.start()
    load_rows.start()
    load_cols.wait()
    count = jnp.int32(0)
    for occ in range(OCC):
        live = occ_live[tile, occ]

        @pl.when(live != 0)
        def _():
            flipped = cols[:, occ * TS:(occ + 1) * TS].astype(F32).T.astype(BF)
            coeffs[jnp.minimum(count, LIVE - 1)] = jnp.where(core == 0, flipped[:HALF], flipped[HALF:])

        count = count + jnp.where(live != 0, 1, 0)
    row = lax.broadcasted_iota(jnp.int32, (TS, TS), 0)
    col = lax.broadcasted_iota(jnp.int32, (TS, TS), 1)
    block_nu = TS // AUXROWS
    perm = (col == (row % block_nu) * AUXROWS + row // block_nu).astype(BF)
    load_rows.wait()
    for out, part in ((give, 1 - core), (keep, core)):
        for j in range(2):
            for quarter in range(AUXROWS):
                start = pl.multiple_of(((part * 2 + j) * AUXROWS + quarter) * TS, TS)
                mixed = jnp.dot(perm, rows[pl.ds(start, TS), :], preferred_element_type=F32).astype(BF)
                for aux in range(AUXROWS):
                    out[aux, j, pl.ds(quarter * block_nu, block_nu), :] = mixed[aux * block_nu:(aux + 1) * block_nu]


def prep(pos, occ_live, eri, orb):
    piece = jax.ShapeDtypeStruct((AUXROWS, 2, TS, TS), BF)
    return pl.pallas_call(
        prep_kernel,
        out_shape=(piece, piece, jax.ShapeDtypeStruct((LIVE, HALF, TS), BF)),
        in_specs=[SMEM, SMEM, ANY, ANY],
        out_specs=(VMEM, VMEM, VMEM),
        scratch_shapes=[
            pltpu.VMEM(eri.shape, BF),
            pltpu.VMEM(orb.shape, BF),
            pltpu.SemaphoreType.DMA((2,)),
        ],
        compiler_params=pltpu.CompilerParams(vmem_limit_bytes=16 * 2**20),
        name="prep",
    )(pos, occ_live, eri, orb)


def main_kernel(pos, pair_tiles, pair_live, occ_index, *refs):
    inputs, (keep, send), scratch = refs[:11], refs[11:13], refs[13:]
    held, (dense, field, block, sems) = scratch[:11], scratch[11:]
    core, x = pos[1], pos[3]
    loads = [pltpu.make_async_copy(src, dst, sems.at[i]) for i, (src, dst) in enumerate(zip(inputs, held))]
    for load in loads:
        load.start()
    coeffs, own0, own_r, own_l, own_r2, own_l2, oth0, oth_r, oth_l, oth_r2, oth_l2 = held

    def clear(tile, carry):
        dense[tile] = jnp.zeros(dense.shape[1:], BF)
        return carry

    lax.fori_loop(0, TILES, clear, 0, unroll=4)
    loads[0].wait()

    def place(tile, carry):
        for k in range(LIVE):
            start = pl.multiple_of(occ_index[tile, k] * HALF, HALF)
            dense[tile, pl.ds(start, HALF), :] = coeffs[tile // NX, tile % NX, k]
        return carry

    lax.fori_loop(0, TILES, place, 0, unroll=4)

    def transform(xp, own, oth, lo, count):
        def body(step, carry):
            tile = (lo + step) * NX + xp
            lhs, rhs = [], []
            for part, ref in ((core, own), (1 - core, oth)):
                for j in range(2):
                    slot = part * 2 + j
                    eri = ref[step, j]
                    rhs.append(jnp.where(pair_live[tile, slot] != 0, eri, jnp.zeros_like(eri)))
                    lhs.append(dense[pair_tiles[tile, slot]])
            half = jnp.dot(
                jnp.concatenate(lhs, axis=1), jnp.concatenate(rhs, axis=0), preferred_element_type=F32
            )
            field[tile] = half.astype(BF)
            return carry

        lax.fori_loop(0, count, body, 0, unroll=4)

    for own, oth, xp, lo, count, first in (
        (own0, oth0, x, 0, 8, 1),
        (own_r, oth_r, (x + 3) % NX, 0, 8, 2),
        (own_l, oth_l, (x + 1) % NX, 0, 8, 3),
        (own_r2, oth_r2, (x + 2) % NX, 0, 4, 4),
        (own_l2, oth_l2, (x + 2) % NX, 4, 4, 5),
    ):
        loads[first].wait()
        loads[first + 5].wait()
        transform(xp, own, oth, lo, count)

    def gram(zp, carry):
        tile = zp * NX + x
        partners = jnp.concatenate([field[pair_tiles[tile, slot]] for slot in range(SLOTS)], axis=1)
        block[...] = lax.dot_general(
            field[tile], partners, (((0,), (0,)), ((), ())), preferred_element_type=F32
        )
        for y in range(NY):
            near = pl.multiple_of(y * 2 * ROWS + core * ROWS, ROWS)
            far = pl.multiple_of(y * 2 * ROWS + (1 - core) * ROWS, ROWS)
            for slot in range(SLOTS):
                keep[y, zp, slot] = block[pl.ds(near, ROWS), slot * TS:(slot + 1) * TS]
                send[y, zp, slot] = block[pl.ds(far, ROWS), slot * TS:(slot + 1) * TS]
        return carry

    lax.fori_loop(0, NZ, gram, 0)


def exchange(pos, pair_tiles, pair_live, occ_index, *pieces):
    shape = jax.ShapeDtypeStruct((NY, NZ, SLOTS, ROWS, TS), F32)
    return pl.pallas_call(
        main_kernel,
        out_shape=(shape, shape),
        in_specs=[SMEM] * 4 + [ANY] * len(pieces),
        out_specs=(VMEM, VMEM),
        scratch_shapes=[pltpu.VMEM(piece.shape, BF) for piece in pieces] + [
            pltpu.VMEM((TILES, OCC * HALF, TS), BF),
            pltpu.VMEM((TILES, OCC * HALF, TS), BF),
            pltpu.VMEM((TS, SLOTS * TS), F32),
            pltpu.SemaphoreType.DMA((len(pieces),)),
        ],
        compiler_params=pltpu.CompilerParams(vmem_limit_bytes=40 * 2**20),
        name="exchange",
    )(pos, pair_tiles, pair_live, occ_index, *pieces)


def shift(value, axis, size, by):
    return lax.ppermute(value, axis, [(i, (i + by) % size) for i in range(size)])


def swap(value):
    return lax.ppermute(value, "c", [(0, 1), (1, 0)])


def shards(integrals, orbitals, pair_tiles, pair_live, occ_live):
    pos = jnp.stack([lax.axis_index(name).astype(jnp.int32) for name in ("y", "c", "z", "x")])
    tile = pos[2] * NX + pos[3]
    eri = integrals.reshape(SLOTS * TS * AUXROWS, TS)
    keep_eri, give_eri, coeffs = prep(pos, occ_live, eri, orbitals)
    rank = jnp.cumsum(occ_live, axis=1) - 1
    hits = (occ_live[:, :, None] != 0) & (rank[:, :, None] == jnp.arange(LIVE)[None, None, :])
    occ_index = jnp.sum(jnp.where(hits, jnp.arange(OCC)[None, :, None], 0), axis=1).astype(jnp.int32)

    row_coeffs = lax.all_gather(coeffs, "x", axis=0)
    all_coeffs = lax.all_gather(row_coeffs, "z", axis=0)

    got_eri = swap(give_eri)
    by_aux = lax.dynamic_slice_in_dim(
        jnp.concatenate([keep_eri, got_eri, keep_eri]), pos[1] * AUXROWS, NZ, 0
    )
    own0 = lax.all_to_all(by_aux, "z", split_axis=0, concat_axis=0, tiled=True)
    own_r, own_l = shift(own0, "x", NX, 1), shift(own0, "x", NX, -1)
    oth0 = swap(own0)
    own_r2, own_l2 = shift(own_r[:4], "x", NX, 1), shift(own_l[4:], "x", NX, -1)
    oth_r, oth_l = swap(own_r), swap(own_l)
    oth_r2, oth_l2 = swap(own_r2), swap(own_l2)

    keep, send = exchange(
        pos, pair_tiles, pair_live, occ_index,
        all_coeffs, own0, own_r, own_l, own_r2, own_l2, oth0, oth_r, oth_l, oth_r2, oth_l2,
    )
    partial = (keep + swap(send)).astype(BF).reshape(NY * NZ, SLOTS, ROWS, TS)
    parts = lax.all_to_all(partial, ("y", "z"), split_axis=0, concat_axis=0, tiled=True).astype(F32)
    flags = lax.dynamic_index_in_dim(pair_live, tile, 0, keepdims=False).astype(F32) * SCALE
    return (jnp.sum(parts, axis=0) * flags[:, None, None])[None]


def solution(mesh):
    grid = Mesh(mesh.devices.reshape(NY, NC, NZ, NX), ("y", "c", "z", "x"))
    return jax.shard_map(
        shards,
        mesh=grid,
        in_specs=(
            P(("z", "x"), None, None, ("y", "c"), None),
            P(("z", "x"), None),
            P(),
            P(),
            P(),
        ),
        out_specs=P(("z", "x"), None, ("y", "c"), None),
        check_vma=False,
    )
```

```python
import functools
import math

import jax
import jax.numpy as jnp
from jax import lax
from jax.experimental import pallas as pl
from jax.experimental.pallas import tpu as pltpu
from jax.sharding import Mesh, PartitionSpec as P

NY, NC, NZ, NX = 4, 2, 8, 4
TILES, SLOTS, TS = 32, 4, 128
OCC, LIVE = 8, 4
AUXROWS = 4
HALF = TS // 2
ROWS = TS // (NY * NC)
SCALE = 1.0 / math.sqrt(32768.0)
BF = jnp.bfloat16
F32 = jnp.float32
VMEM = pl.BlockSpec(memory_space=pltpu.VMEM)
SMEM = pl.BlockSpec(memory_space=pltpu.SMEM)
ANY = pl.BlockSpec(memory_space=pl.ANY)


def prep_kernel(pos, occ_live, eri, orb, keep, give, coeffs, rows, cols, sems):
    slab, core, tile = pos[0], pos[1], pos[2] * NX + pos[3]
    load_cols = pltpu.make_async_copy(orb, cols, sems.at[0])
    load_rows = pltpu.make_async_copy(eri, rows, sems.at[1])
    load_cols.start()
    load_rows.start()
    load_cols.wait()
    count = jnp.int32(0)
    for occ in range(OCC):
        live = occ_live[occ, tile] != 0

        @pl.when(live & (count == slab))
        def _():
            flipped = cols[:, occ * TS:(occ + 1) * TS].astype(F32).T.astype(BF)
            coeffs[...] = jnp.where(core == 0, flipped[:HALF], flipped[HALF:])

        count = count + jnp.where(live, 1, 0)
    row = lax.broadcasted_iota(jnp.int32, (TS, TS), 0)
    col = lax.broadcasted_iota(jnp.int32, (TS, TS), 1)
    block_nu = TS // AUXROWS
    perm = (col == (row % block_nu) * AUXROWS + row // block_nu).astype(BF)
    load_rows.wait()
    for out, part in ((give, 1 - core), (keep, core)):
        for j in range(2):
            for quarter in range(AUXROWS):
                start = pl.multiple_of(((part * 2 + j) * AUXROWS + quarter) * TS, TS)
                mixed = jnp.dot(perm, rows[pl.ds(start, TS), :], preferred_element_type=F32).astype(BF)
                for aux in range(AUXROWS):
                    out[aux, j, pl.ds(quarter * block_nu, block_nu), :] = mixed[aux * block_nu:(aux + 1) * block_nu]


def prep(pos, occ_live, eri, orb):
    piece = jax.ShapeDtypeStruct((AUXROWS, 2, TS, TS), BF)
    return pl.pallas_call(
        prep_kernel,
        out_shape=(piece, piece, jax.ShapeDtypeStruct((HALF, TS), BF)),
        in_specs=[SMEM, SMEM, ANY, ANY],
        out_specs=(VMEM, VMEM, VMEM),
        scratch_shapes=[
            pltpu.VMEM(eri.shape, BF),
            pltpu.VMEM(orb.shape, BF),
            pltpu.SemaphoreType.DMA((2,)),
        ],
        compiler_params=pltpu.CompilerParams(vmem_limit_bytes=56 * 2**20),
        name="prep",
    )(pos, occ_live, eri, orb)


def main_kernel(pos, pair_tiles, pair_live, occ_index, *refs):
    inputs, (keep, send), scratch = refs[:15], refs[15:17], refs[17:]
    held, (dense, field, block, sems) = scratch[:15], scratch[15:]
    slab, core, x = pos[0], pos[1], pos[3]
    loads = [pltpu.make_async_copy(src, dst, sems.at[i]) for i, (src, dst) in enumerate(zip(inputs, held))]
    for load in loads:
        load.start()
    c0, c_u, c_d, c_u2, c_d2, own0, own_r, own_l, own_r2, own_l2, oth0, oth_r, oth_l, oth_r2, oth_l2 = held

    def clear(tile, carry):
        dense[tile] = jnp.zeros(dense.shape[1:], BF)
        return carry

    lax.fori_loop(0, TILES, clear, 0, unroll=4)

    def place(piece, k, lo, count):
        def body(step, carry):
            for entry in range(NX):
                tile = (lo + step) * NX + (x - entry + NX) % NX
                start = pl.multiple_of(occ_index[k, tile] * HALF, HALF)
                dense[tile, pl.ds(start, HALF), :] = piece[step, entry]
            return carry

        lax.fori_loop(0, count, body, 0, unroll=True)

    for index, (piece, k, lo, count) in enumerate((
        (c0, slab, 0, 8),
        (c_u, (slab + 3) % NY, 0, 8),
        (c_d, (slab + 1) % NY, 0, 8),
        (c_u2, (slab + 2) % NY, 0, 4),
        (c_d2, (slab + 2) % NY, 4, 4),
    )):
        loads[index].wait()
        place(piece, k, lo, count)

    def transform(xp, own, oth, lo, count):
        def body(step, carry):
            tile = (lo + step) * NX + xp
            lhs, rhs = [], []
            for part, ref in ((core, own), (1 - core, oth)):
                for j in range(2):
                    slot = part * 2 + j
                    eri = ref[step, j]
                    rhs.append(jnp.where(pair_live[slot, tile] != 0, eri, jnp.zeros_like(eri)))
                    lhs.append(dense[pair_tiles[slot, tile]])
            half = jnp.dot(
                jnp.concatenate(lhs, axis=1), jnp.concatenate(rhs, axis=0), preferred_element_type=F32
            )
            field[tile] = half.astype(BF)
            return carry

        lax.fori_loop(0, count, body, 0, unroll=4)

    for own, oth, xp, lo, count, first in (
        (own0, oth0, x, 0, 8, 5),
        (own_r, oth_r, (x + 3) % NX, 0, 8, 6),
        (own_l, oth_l, (x + 1) % NX, 0, 8, 7),
        (own_r2, oth_r2, (x + 2) % NX, 0, 4, 8),
        (own_l2, oth_l2, (x + 2) % NX, 4, 4, 9),
    ):
        loads[first].wait()
        loads[first + 5].wait()
        transform(xp, own, oth, lo, count)

    def gram(zp, carry):
        tile = zp * NX + x
        partners = jnp.concatenate([field[pair_tiles[slot, tile]] for slot in range(SLOTS)], axis=1)
        block[...] = lax.dot_general(
            field[tile], partners, (((0,), (0,)), ((), ())), preferred_element_type=F32
        )
        for y in range(NY):
            near = pl.multiple_of(y * 2 * ROWS + core * ROWS, ROWS)
            far = pl.multiple_of(y * 2 * ROWS + (1 - core) * ROWS, ROWS)
            for slot in range(SLOTS):
                keep[y, zp, slot] = block[pl.ds(near, ROWS), slot * TS:(slot + 1) * TS]
                send[y, zp, slot] = block[pl.ds(far, ROWS), slot * TS:(slot + 1) * TS]
        return carry

    lax.fori_loop(0, NZ, gram, 0)


def exchange(pos, pair_tiles, pair_live, occ_index, *pieces):
    shape = jax.ShapeDtypeStruct((NY, NZ, SLOTS, ROWS, TS), F32)
    return pl.pallas_call(
        main_kernel,
        out_shape=(shape, shape),
        in_specs=[SMEM] * 4 + [ANY] * len(pieces),
        out_specs=(VMEM, VMEM),
        scratch_shapes=[pltpu.VMEM(piece.shape, BF) for piece in pieces] + [
            pltpu.VMEM((TILES, OCC * HALF, TS), BF),
            pltpu.VMEM((TILES, OCC * HALF, TS), BF),
            pltpu.VMEM((TS, SLOTS * TS), F32),
            pltpu.SemaphoreType.DMA((len(pieces),)),
        ],
        compiler_params=pltpu.CompilerParams(vmem_limit_bytes=56 * 2**20),
        name="exchange",
    )(pos, pair_tiles, pair_live, occ_index, *pieces)


def shift(value, axis, size, by):
    return lax.ppermute(value, axis, [(i, (i + by) % size) for i in range(size)])


def swap(value):
    return lax.ppermute(value, "c", [(0, 1), (1, 0)])


def shards(integrals, orbitals, pair_tiles, pair_live, occ_live):
    pos = jnp.stack([lax.axis_index(name).astype(jnp.int32) for name in ("y", "c", "z", "x")])
    tile = pos[2] * NX + pos[3]
    eri = integrals.reshape(SLOTS * TS * AUXROWS, TS)
    keep_eri, give_eri, coeffs = prep(pos, occ_live.T, eri, orbitals)
    rank = jnp.cumsum(occ_live, axis=1) - 1
    hits = (occ_live[None] != 0) & (rank[None] == jnp.arange(LIVE)[:, None, None])
    occ_index = jnp.sum(jnp.where(hits, jnp.arange(OCC)[None, None, :], 0), axis=2).astype(jnp.int32)

    got_eri = swap(give_eri)
    row_coeffs = jnp.stack([coeffs] + [shift(coeffs, "x", NX, by) for by in (1, 2, 3)])
    got_eri, row_coeffs = lax.optimization_barrier((got_eri, row_coeffs))
    by_aux = lax.dynamic_slice_in_dim(
        jnp.concatenate([keep_eri, got_eri, keep_eri]), pos[1] * AUXROWS, NZ, 0
    )
    own0 = lax.all_to_all(by_aux, "z", split_axis=0, concat_axis=0, tiled=True)
    c0 = lax.all_gather(row_coeffs, "z", axis=0)
    own0, c0 = lax.optimization_barrier((own0, c0))
    own_r, own_l = shift(own0, "x", NX, 1), shift(own0, "x", NX, -1)
    c_u, c_d = shift(c0, "y", NY, 1), shift(c0, "y", NY, -1)
    oth0 = swap(own0)
    own_r2, own_l2 = shift(own_r[:4], "x", NX, 1), shift(own_l[4:], "x", NX, -1)
    c_u2, c_d2 = shift(c_u[:4], "y", NY, 1), shift(c_d[4:], "y", NY, -1)
    oth_r, oth_l = swap(own_r), swap(own_l)
    oth_r2, oth_l2 = swap(own_r2), swap(own_l2)

    keep, send = exchange(
        pos, pair_tiles.T, pair_live.T, occ_index,
        c0, c_u, c_d, c_u2, c_d2, own0, own_r, own_l, own_r2, own_l2, oth0, oth_r, oth_l, oth_r2, oth_l2,
    )
    partial = (keep + swap(send)).astype(BF).reshape(NY * NZ, SLOTS, ROWS, TS)
    parts = lax.all_to_all(partial, ("y", "z"), split_axis=0, concat_axis=0, tiled=True).astype(F32)
    flags = lax.dynamic_index_in_dim(pair_live, tile, 0, keepdims=False).astype(F32) * SCALE
    return (jnp.sum(parts, axis=0) * flags[:, None, None])[None]


def solution(mesh):
    grid = Mesh(mesh.devices.reshape(NY, NC, NZ, NX), ("y", "c", "z", "x"))
    return jax.shard_map(
        shards,
        mesh=grid,
        in_specs=(
            P(("z", "x"), None, None, ("y", "c"), None),
            P(("z", "x"), None),
            P(),
            P(),
            P(),
        ),
        out_specs=P(("z", "x"), None, ("y", "c"), None),
        check_vma=False,
    )
```

```python
import functools
import math

import jax
import jax.numpy as jnp
from jax import lax
from jax.experimental import pallas as pl
from jax.experimental.pallas import tpu as pltpu
from jax.sharding import Mesh, PartitionSpec as P

NY, NC, NZ, NX = 4, 2, 8, 4
TILES, SLOTS, TS = 32, 4, 128
OCC, LIVE = 8, 4
AUXROWS = 4
HALF = TS // 2
ROWS = TS // (NY * NC)
SCALE = 1.0 / math.sqrt(32768.0)
BF = jnp.bfloat16
F32 = jnp.float32
VMEM = pl.BlockSpec(memory_space=pltpu.VMEM)
SMEM = pl.BlockSpec(memory_space=pltpu.SMEM)
ANY = pl.BlockSpec(memory_space=pl.ANY)
HBM = pl.BlockSpec(memory_space=pltpu.HBM)


def prep_kernel(pos, occ_live, eri, orb, keep, give, coeffs, rows, cols, sems):
    slab, core, tile = pos[0], pos[1], pos[2] * NX + pos[3]
    load_cols = pltpu.make_async_copy(orb, cols, sems.at[0])
    size = 2 * AUXROWS * TS
    loads = []
    for index, part in enumerate((1 - core, core)):
        span = pl.ds(pl.multiple_of(part * size, size), size)
        loads.append(pltpu.make_async_copy(eri.at[span], rows.at[span], sems.at[index + 1]))
    load_cols.start()
    for load in loads:
        load.start()
    load_cols.wait()
    count = jnp.int32(0)
    for occ in range(OCC):
        live = occ_live[occ, tile] != 0

        @pl.when(live & (count == slab))
        def _():
            flipped = cols[:, occ * TS:(occ + 1) * TS].astype(F32).T.astype(BF)
            coeffs[...] = jnp.where(core == 0, flipped[:HALF], flipped[HALF:])

        count = count + jnp.where(live, 1, 0)
    row = lax.broadcasted_iota(jnp.int32, (TS, TS), 0)
    col = lax.broadcasted_iota(jnp.int32, (TS, TS), 1)
    block_nu = TS // AUXROWS
    perm = (col == (row % block_nu) * AUXROWS + row // block_nu).astype(BF)
    for out, part, load in ((give, 1 - core, loads[0]), (keep, core, loads[1])):
        load.wait()
        for j in range(2):
            for quarter in range(AUXROWS):
                start = pl.multiple_of(((part * 2 + j) * AUXROWS + quarter) * TS, TS)
                mixed = jnp.dot(perm, rows[pl.ds(start, TS), :], preferred_element_type=F32).astype(BF)
                for aux in range(AUXROWS):
                    out[aux, j, pl.ds(quarter * block_nu, block_nu), :] = mixed[aux * block_nu:(aux + 1) * block_nu]


def prep(pos, occ_live, eri, orb):
    piece = jax.ShapeDtypeStruct((AUXROWS, 2, TS, TS), BF)
    return pl.pallas_call(
        prep_kernel,
        out_shape=(piece, piece, jax.ShapeDtypeStruct((HALF, TS), BF)),
        in_specs=[SMEM, SMEM, HBM, HBM],
        out_specs=(VMEM, VMEM, VMEM),
        scratch_shapes=[
            pltpu.VMEM(eri.shape, BF),
            pltpu.VMEM(orb.shape, BF),
            pltpu.SemaphoreType.DMA((3,)),
        ],
        compiler_params=pltpu.CompilerParams(vmem_limit_bytes=8 * 2**20),
        name="prep",
    )(pos, occ_live, eri, orb)


def main_kernel(pos, pair_tiles, pair_live, occ_index, *refs):
    inputs, (keep, send), scratch = refs[:15], refs[15:17], refs[17:]
    held, (dense, field, block, sems) = scratch[:15], scratch[15:]
    slab, core, x = pos[0], pos[1], pos[3]
    loads = [pltpu.make_async_copy(src, dst, sems.at[i]) for i, (src, dst) in enumerate(zip(inputs, held))]
    for load in loads:
        load.start()
    c0, c_u, c_d, c_u2, c_d2, own0, own_r, own_l, own_r2, own_l2, oth0, oth_r, oth_l, oth_r2, oth_l2 = held

    def clear(tile, carry):
        dense[tile] = jnp.zeros(dense.shape[1:], BF)
        return carry

    lax.fori_loop(0, TILES, clear, 0, unroll=4)

    def place(piece, k, lo, count):
        def body(step, carry):
            for entry in range(NX):
                tile = (lo + step) * NX + (x - entry + NX) % NX
                start = pl.multiple_of(occ_index[k, tile] * HALF, HALF)
                dense[tile, pl.ds(start, HALF), :] = piece[step, entry]
            return carry

        lax.fori_loop(0, count, body, 0, unroll=True)

    for index, (piece, k, lo, count) in enumerate((
        (c0, slab, 0, 8),
        (c_u, (slab + 3) % NY, 0, 8),
        (c_d, (slab + 1) % NY, 0, 8),
        (c_u2, (slab + 2) % NY, 0, 4),
        (c_d2, (slab + 2) % NY, 4, 4),
    )):
        loads[index].wait()
        place(piece, k, lo, count)

    def transform(xp, own, oth, lo, count):
        def body(step, carry):
            tile = (lo + step) * NX + xp
            lhs, rhs = [], []
            for part, ref in ((core, own), (1 - core, oth)):
                for j in range(2):
                    slot = part * 2 + j
                    eri = ref[step, j]
                    rhs.append(jnp.where(pair_live[slot, tile] != 0, eri, jnp.zeros_like(eri)))
                    lhs.append(dense[pair_tiles[slot, tile]])
            half = jnp.dot(
                jnp.concatenate(lhs, axis=1), jnp.concatenate(rhs, axis=0), preferred_element_type=F32
            )
            field[tile] = half.astype(BF)
            return carry

        lax.fori_loop(0, count, body, 0, unroll=4)

    for own, oth, xp, lo, count, first in (
        (own0, oth0, x, 0, 8, 5),
        (own_r, oth_r, (x + 3) % NX, 0, 8, 6),
        (own_l, oth_l, (x + 1) % NX, 0, 8, 7),
        (own_r2, oth_r2, (x + 2) % NX, 0, 4, 8),
        (own_l2, oth_l2, (x + 2) % NX, 4, 4, 9),
    ):
        loads[first].wait()
        loads[first + 5].wait()
        transform(xp, own, oth, lo, count)

    def gram(zp, carry):
        tile = zp * NX + x
        partners = jnp.concatenate([field[pair_tiles[slot, tile]] for slot in range(SLOTS)], axis=1)
        block[...] = lax.dot_general(
            field[tile], partners, (((0,), (0,)), ((), ())), preferred_element_type=F32
        )
        for y in range(NY):
            near = pl.multiple_of(y * 2 * ROWS + core * ROWS, ROWS)
            far = pl.multiple_of(y * 2 * ROWS + (1 - core) * ROWS, ROWS)
            for slot in range(SLOTS):
                keep[y, zp, slot] = block[pl.ds(near, ROWS), slot * TS:(slot + 1) * TS]
                send[y, zp, slot] = block[pl.ds(far, ROWS), slot * TS:(slot + 1) * TS]
        return carry

    lax.fori_loop(0, NZ, gram, 0)


def exchange(pos, pair_tiles, pair_live, occ_index, *pieces):
    shape = jax.ShapeDtypeStruct((NY, NZ, SLOTS, ROWS, TS), F32)
    return pl.pallas_call(
        main_kernel,
        out_shape=(shape, shape),
        in_specs=[SMEM] * 4 + [ANY] * len(pieces),
        out_specs=(VMEM, VMEM),
        scratch_shapes=[pltpu.VMEM(piece.shape, BF) for piece in pieces] + [
            pltpu.VMEM((TILES, OCC * HALF, TS), BF),
            pltpu.VMEM((TILES, OCC * HALF, TS), BF),
            pltpu.VMEM((TS, SLOTS * TS), F32),
            pltpu.SemaphoreType.DMA((len(pieces),)),
        ],
        compiler_params=pltpu.CompilerParams(vmem_limit_bytes=24 * 2**20),
        name="exchange",
    )(pos, pair_tiles, pair_live, occ_index, *pieces)


def shift(value, axis, size, by):
    return lax.ppermute(value, axis, [(i, (i + by) % size) for i in range(size)])


def swap(value):
    return lax.ppermute(value, "c", [(0, 1), (1, 0)])


def shards(integrals, orbitals, pair_tiles, pair_live, occ_live):
    pos = jnp.stack([lax.axis_index(name).astype(jnp.int32) for name in ("y", "c", "z", "x")])
    tile = pos[2] * NX + pos[3]
    eri = integrals.reshape(SLOTS * TS * AUXROWS, TS)
    keep_eri, give_eri, coeffs = prep(pos, occ_live.T, eri, orbitals)
    rank = jnp.cumsum(occ_live, axis=1) - 1
    hits = (occ_live[None] != 0) & (rank[None] == jnp.arange(LIVE)[:, None, None])
    occ_index = jnp.sum(jnp.where(hits, jnp.arange(OCC)[None, None, :], 0), axis=2).astype(jnp.int32)

    got_eri = swap(give_eri)
    row_coeffs = jnp.stack([coeffs] + [shift(coeffs, "x", NX, by) for by in (1, 2, 3)])
    by_aux = lax.dynamic_slice_in_dim(
        jnp.concatenate([keep_eri, got_eri, keep_eri]), pos[1] * AUXROWS, NZ, 0
    )
    outgoing = jnp.concatenate([
        by_aux.reshape(NZ, 2 * TS, TS),
        jnp.broadcast_to(row_coeffs.reshape(1, NX * HALF, TS), (NZ, NX * HALF, TS)),
    ], axis=1)
    arrived = lax.all_to_all(outgoing, "z", split_axis=0, concat_axis=0, tiled=True)
    own0 = arrived[:, :2 * TS].reshape(NZ, 2, TS, TS)
    c0 = arrived[:, 2 * TS:].reshape(NZ, NX, HALF, TS)
    own0, c0 = lax.optimization_barrier((own0, c0))
    own_r, own_l = shift(own0, "x", NX, 1), shift(own0, "x", NX, -1)
    c_u, c_d = shift(c0, "y", NY, 1), shift(c0, "y", NY, -1)
    oth0 = swap(own0)
    own_r2, own_l2 = shift(own_r[:4], "x", NX, 1), shift(own_l[4:], "x", NX, -1)
    c_u2, c_d2 = shift(c_u[:4], "y", NY, 1), shift(c_d[4:], "y", NY, -1)
    oth_r, oth_l = swap(own_r), swap(own_l)
    oth_r2, oth_l2 = swap(own_r2), swap(own_l2)

    keep, send = exchange(
        pos, pair_tiles.T, pair_live.T, occ_index,
        c0, c_u, c_d, c_u2, c_d2, own0, own_r, own_l, own_r2, own_l2, oth0, oth_r, oth_l, oth_r2, oth_l2,
    )
    partial = (keep + swap(send)).astype(BF).reshape(NY * NZ, SLOTS, ROWS, TS)
    parts = lax.all_to_all(partial, ("y", "z"), split_axis=0, concat_axis=0, tiled=True).astype(F32)
    flags = lax.dynamic_index_in_dim(pair_live, tile, 0, keepdims=False).astype(F32) * SCALE
    return (jnp.sum(parts, axis=0) * flags[:, None, None])[None]


def solution(mesh):
    grid = Mesh(mesh.devices.reshape(NY, NC, NZ, NX), ("y", "c", "z", "x"))
    return jax.shard_map(
        shards,
        mesh=grid,
        in_specs=(
            P(("z", "x"), None, None, ("y", "c"), None),
            P(("z", "x"), None),
            P(),
            P(),
            P(),
        ),
        out_specs=P(("z", "x"), None, ("y", "c"), None),
        check_vma=False,
    )
```

```python
import functools
import math

import jax
import jax.numpy as jnp
from jax import lax
from jax.experimental import pallas as pl
from jax.experimental.pallas import tpu as pltpu
from jax.sharding import Mesh, PartitionSpec as P

NY, NC, NZ, NX = 4, 2, 8, 4
TILES, SLOTS, TS = 32, 4, 128
OCC, LIVE = 8, 4
AUXROWS = 4
HALF = TS // 2
ROWS = TS // (NY * NC)
SCALE = 1.0 / math.sqrt(32768.0)
BF = jnp.bfloat16
F32 = jnp.float32
VMEM = pl.BlockSpec(memory_space=pltpu.VMEM)
SMEM = pl.BlockSpec(memory_space=pltpu.SMEM)
ANY = pl.BlockSpec(memory_space=pl.ANY)
HBM = pl.BlockSpec(memory_space=pltpu.HBM)


def prep_kernel(pos, occ_live, eri, orb, keep, give, coeffs, rows, cols, sems):
    slab, core, tile = pos[0], pos[1], pos[2] * NX + pos[3]
    load_cols = pltpu.make_async_copy(orb, cols, sems.at[0])
    size = 2 * AUXROWS * TS
    loads = []
    for index, part in enumerate((1 - core, core)):
        span = pl.ds(pl.multiple_of(part * size, size), size)
        loads.append(pltpu.make_async_copy(eri.at[span], rows.at[span], sems.at[index + 1]))
    load_cols.start()
    for load in loads:
        load.start()
    load_cols.wait()
    count = jnp.int32(0)
    for occ in range(OCC):
        live = occ_live[occ, tile] != 0

        @pl.when(live & (count == slab))
        def _():
            flipped = cols[:, occ * TS:(occ + 1) * TS].astype(F32).T.astype(BF)
            mine = jnp.where(core == 0, flipped[:HALF], flipped[HALF:])
            for target in range(NZ):
                coeffs[target] = mine

        count = count + jnp.where(live, 1, 0)
    row = lax.broadcasted_iota(jnp.int32, (TS, TS), 0)
    col = lax.broadcasted_iota(jnp.int32, (TS, TS), 1)
    block_nu = TS // AUXROWS
    perm = (col == (row % block_nu) * AUXROWS + row // block_nu).astype(BF)
    for out, part, load in ((give, 1 - core, loads[0]), (keep, core, loads[1])):
        load.wait()
        for j in range(2):
            for quarter in range(AUXROWS):
                start = pl.multiple_of(((part * 2 + j) * AUXROWS + quarter) * TS, TS)
                mixed = jnp.dot(perm, rows[pl.ds(start, TS), :], preferred_element_type=F32).astype(BF)
                for aux in range(AUXROWS):
                    out[aux, j, pl.ds(quarter * block_nu, block_nu), :] = mixed[aux * block_nu:(aux + 1) * block_nu]


def prep(pos, occ_live, eri, orb):
    piece = jax.ShapeDtypeStruct((AUXROWS, 2, TS, TS), BF)
    return pl.pallas_call(
        prep_kernel,
        out_shape=(piece, piece, jax.ShapeDtypeStruct((NZ, HALF, TS), BF)),
        in_specs=[SMEM, SMEM, HBM, HBM],
        out_specs=(VMEM, VMEM, VMEM),
        scratch_shapes=[
            pltpu.VMEM(eri.shape, BF),
            pltpu.VMEM(orb.shape, BF),
            pltpu.SemaphoreType.DMA((3,)),
        ],
        compiler_params=pltpu.CompilerParams(vmem_limit_bytes=8 * 2**20),
        name="prep",
    )(pos, occ_live, eri, orb)


def main_kernel(pos, pair_tiles, pair_live, occ_index, *refs):
    inputs, (keep, send), scratch = refs[:15], refs[15:17], refs[17:]
    held, (dense, field, block, sems) = scratch[:15], scratch[15:]
    slab, core, x = pos[0], pos[1], pos[3]
    loads = [pltpu.make_async_copy(src, dst, sems.at[i]) for i, (src, dst) in enumerate(zip(inputs, held))]
    for load in loads:
        load.start()
    c0, c_u, c_d, c_u2, c_d2, own0, own_r, own_l, own_r2, own_l2, oth0, oth_r, oth_l, oth_r2, oth_l2 = held

    def clear(tile, carry):
        dense[tile] = jnp.zeros(dense.shape[1:], BF)
        return carry

    lax.fori_loop(0, TILES, clear, 0, unroll=4)

    def place(piece, k, lo, count):
        def body(step, carry):
            for entry in range(NX):
                tile = (lo + step) * NX + (x - entry + NX) % NX
                start = pl.multiple_of(occ_index[k, tile] * HALF, HALF)
                dense[tile, pl.ds(start, HALF), :] = piece[step, entry]
            return carry

        lax.fori_loop(0, count, body, 0, unroll=True)

    for index, (piece, k, lo, count) in enumerate((
        (c0, slab, 0, 8),
        (c_u, (slab + 3) % NY, 0, 8),
        (c_d, (slab + 1) % NY, 0, 8),
        (c_u2, (slab + 2) % NY, 0, 4),
        (c_d2, (slab + 2) % NY, 4, 4),
    )):
        loads[index].wait()
        place(piece, k, lo, count)

    def transform(xp, own, oth, lo, count):
        def body(step, carry):
            tile = (lo + step) * NX + xp
            lhs, rhs = [], []
            for part, ref in ((core, own), (1 - core, oth)):
                for j in range(2):
                    slot = part * 2 + j
                    eri = ref[step, j]
                    rhs.append(jnp.where(pair_live[slot, tile] != 0, eri, jnp.zeros_like(eri)))
                    lhs.append(dense[pair_tiles[slot, tile]])
            half = jnp.dot(
                jnp.concatenate(lhs, axis=1), jnp.concatenate(rhs, axis=0), preferred_element_type=F32
            )
            field[tile] = half.astype(BF)
            return carry

        lax.fori_loop(0, count, body, 0, unroll=4)

    for own, oth, xp, lo, count, first in (
        (own0, oth0, x, 0, 8, 5),
        (own_r, oth_r, (x + 3) % NX, 0, 8, 6),
        (own_l, oth_l, (x + 1) % NX, 0, 8, 7),
        (own_r2, oth_r2, (x + 2) % NX, 0, 4, 8),
        (own_l2, oth_l2, (x + 2) % NX, 4, 4, 9),
    ):
        loads[first].wait()
        loads[first + 5].wait()
        transform(xp, own, oth, lo, count)

    def gram(zp, carry):
        tile = zp * NX + x
        partners = jnp.concatenate([field[pair_tiles[slot, tile]] for slot in range(SLOTS)], axis=1)
        block[...] = lax.dot_general(
            field[tile], partners, (((0,), (0,)), ((), ())), preferred_element_type=F32
        )
        for y in range(NY):
            near = pl.multiple_of(y * 2 * ROWS + core * ROWS, ROWS)
            far = pl.multiple_of(y * 2 * ROWS + (1 - core) * ROWS, ROWS)
            for slot in range(SLOTS):
                keep[y, zp, slot] = block[pl.ds(near, ROWS), slot * TS:(slot + 1) * TS]
                send[y, zp, slot] = block[pl.ds(far, ROWS), slot * TS:(slot + 1) * TS]
        return carry

    lax.fori_loop(0, NZ, gram, 0)


def exchange(pos, pair_tiles, pair_live, occ_index, *pieces):
    shape = jax.ShapeDtypeStruct((NY, NZ, SLOTS, ROWS, TS), F32)
    return pl.pallas_call(
        main_kernel,
        out_shape=(shape, shape),
        in_specs=[SMEM] * 4 + [ANY] * len(pieces),
        out_specs=(VMEM, VMEM),
        scratch_shapes=[pltpu.VMEM(piece.shape, BF) for piece in pieces] + [
            pltpu.VMEM((TILES, OCC * HALF, TS), BF),
            pltpu.VMEM((TILES, OCC * HALF, TS), BF),
            pltpu.VMEM((TS, SLOTS * TS), F32),
            pltpu.SemaphoreType.DMA((len(pieces),)),
        ],
        compiler_params=pltpu.CompilerParams(vmem_limit_bytes=24 * 2**20),
        name="exchange",
    )(pos, pair_tiles, pair_live, occ_index, *pieces)


def shift(value, axis, size, by):
    return lax.ppermute(value, axis, [(i, (i + by) % size) for i in range(size)])


def swap(value):
    return lax.ppermute(value, "c", [(0, 1), (1, 0)])


def shards(integrals, orbitals, pair_tiles, pair_live, occ_live):
    pos = jnp.stack([lax.axis_index(name).astype(jnp.int32) for name in ("y", "c", "z", "x")])
    tile = pos[2] * NX + pos[3]
    eri = integrals.reshape(SLOTS * TS * AUXROWS, TS)
    keep_eri, give_eri, coeffs = prep(pos, occ_live.T, eri, orbitals)
    rank = jnp.cumsum(occ_live, axis=1) - 1
    hits = (occ_live[None] != 0) & (rank[None] == jnp.arange(LIVE)[:, None, None])
    occ_index = jnp.sum(jnp.where(hits, jnp.arange(OCC)[None, None, :], 0), axis=2).astype(jnp.int32)

    got_eri = swap(give_eri)
    column = lax.all_to_all(coeffs, "z", split_axis=0, concat_axis=0, tiled=True)
    got_eri, column = lax.optimization_barrier((got_eri, column))
    by_aux = lax.dynamic_slice_in_dim(
        jnp.concatenate([keep_eri, got_eri, keep_eri]), pos[1] * AUXROWS, NZ, 0
    )
    own0 = lax.all_to_all(by_aux, "z", split_axis=0, concat_axis=0, tiled=True)
    c0 = jnp.stack([column] + [shift(column, "x", NX, by) for by in (1, 2, 3)], axis=1)
    own_r, own_l = shift(own0, "x", NX, 1), shift(own0, "x", NX, -1)
    c_u, c_d = shift(c0, "y", NY, 1), shift(c0, "y", NY, -1)
    oth0 = swap(own0)
    own_r2, own_l2 = shift(own_r[:4], "x", NX, 1), shift(own_l[4:], "x", NX, -1)
    c_u2, c_d2 = shift(c_u[:4], "y", NY, 1), shift(c_d[4:], "y", NY, -1)
    oth_r, oth_l = swap(own_r), swap(own_l)
    oth_r2, oth_l2 = swap(own_r2), swap(own_l2)

    keep, send = exchange(
        pos, pair_tiles.T, pair_live.T, occ_index,
        c0, c_u, c_d, c_u2, c_d2, own0, own_r, own_l, own_r2, own_l2, oth0, oth_r, oth_l, oth_r2, oth_l2,
    )
    partial = (keep + swap(send)).astype(BF).reshape(NY * NZ, SLOTS, ROWS, TS)
    parts = lax.all_to_all(partial, ("y", "z"), split_axis=0, concat_axis=0, tiled=True).astype(F32)
    flags = lax.dynamic_index_in_dim(pair_live, tile, 0, keepdims=False).astype(F32) * SCALE
    return (jnp.sum(parts, axis=0) * flags[:, None, None])[None]


def solution(mesh):
    grid = Mesh(mesh.devices.reshape(NY, NC, NZ, NX), ("y", "c", "z", "x"))
    return jax.shard_map(
        shards,
        mesh=grid,
        in_specs=(
            P(("z", "x"), None, None, ("y", "c"), None),
            P(("z", "x"), None),
            P(),
            P(),
            P(),
        ),
        out_specs=P(("z", "x"), None, ("y", "c"), None),
        check_vma=False,
    )
```

```python
import functools
import math

import jax
import jax.numpy as jnp
from jax import lax
from jax.experimental import pallas as pl
from jax.experimental.pallas import tpu as pltpu
from jax.sharding import Mesh, PartitionSpec as P

NY, NC, NZ, NX = 4, 2, 8, 4
TILES, SLOTS, TS = 32, 4, 128
OCC, LIVE = 8, 4
AUXROWS = 4
HALF = TS // 2
ROWS = TS // (NY * NC)
SCALE = 1.0 / math.sqrt(32768.0)
BF = jnp.bfloat16
F32 = jnp.float32
VMEM = pl.BlockSpec(memory_space=pltpu.VMEM)
SMEM = pl.BlockSpec(memory_space=pltpu.SMEM)
ANY = pl.BlockSpec(memory_space=pl.ANY)


def slice_kernel(pos, occ_live, orb, coeffs, cols, sem):
    slab, core, tile = pos[0], pos[1], pos[2] * NX + pos[3]
    load = pltpu.make_async_copy(orb, cols, sem)
    load.start()
    load.wait()
    count = jnp.int32(0)
    for occ in range(OCC):
        live = occ_live[occ, tile] != 0

        @pl.when(live & (count == slab))
        def _():
            flipped = cols[:, occ * TS:(occ + 1) * TS].astype(F32).T.astype(BF)
            mine = jnp.where(core == 0, flipped[:HALF], flipped[HALF:])
            for target in range(NZ):
                coeffs[target] = mine

        count = count + jnp.where(live, 1, 0)


def slice_coeffs(pos, occ_live, orb):
    return pl.pallas_call(
        slice_kernel,
        out_shape=jax.ShapeDtypeStruct((NZ, HALF, TS), BF),
        in_specs=[SMEM, SMEM, ANY],
        out_specs=VMEM,
        scratch_shapes=[pltpu.VMEM(orb.shape, BF), pltpu.SemaphoreType.DMA],
        compiler_params=pltpu.CompilerParams(vmem_limit_bytes=60 * 2**20),
        cost_estimate=pl.CostEstimate(flops=0, bytes_accessed=2 * orb.size, transcendentals=0),
        name="slice_coeffs",
    )(pos, occ_live, orb)


def split_kernel(pos, eri, keep, give):
    core = pos[1]
    row = lax.broadcasted_iota(jnp.int32, (TS, TS), 0)
    col = lax.broadcasted_iota(jnp.int32, (TS, TS), 1)
    block_nu = TS // AUXROWS
    perm = (col == (row % block_nu) * AUXROWS + row // block_nu).astype(BF)
    for out, part in ((give, 1 - core), (keep, core)):
        for j in range(2):
            for quarter in range(AUXROWS):
                start = pl.multiple_of(((part * 2 + j) * AUXROWS + quarter) * TS, TS)
                mixed = jnp.dot(perm, eri[pl.ds(start, TS), :], preferred_element_type=F32).astype(BF)
                for aux in range(AUXROWS):
                    out[aux, j, pl.ds(quarter * block_nu, block_nu), :] = mixed[aux * block_nu:(aux + 1) * block_nu]


def split_aux(pos, eri):
    piece = jax.ShapeDtypeStruct((AUXROWS, 2, TS, TS), BF)
    return pl.pallas_call(
        split_kernel,
        out_shape=(piece, piece),
        in_specs=[SMEM, VMEM],
        out_specs=(VMEM, VMEM),
        compiler_params=pltpu.CompilerParams(vmem_limit_bytes=8 * 2**20),
        cost_estimate=pl.CostEstimate(flops=2 * TS * eri.size, bytes_accessed=4 * eri.size, transcendentals=0),
        name="split_aux",
    )(pos, eri)


def rebuild_kernel(pos, occ_index, c0, c_u, c_d, c_u2, c_d2, dense):
    slab, x = pos[0], pos[3]

    def clear(tile, carry):
        dense[tile] = jnp.zeros(dense.shape[1:], BF)
        return carry

    lax.fori_loop(0, TILES, clear, 0, unroll=4)

    def place(piece, k, lo, count):
        def body(step, carry):
            for entry in range(NX):
                tile = (lo + step) * NX + (x - entry + NX) % NX
                start = pl.multiple_of(occ_index[k, tile] * HALF, HALF)
                dense[tile, pl.ds(start, HALF), :] = piece[step, entry]
            return carry

        lax.fori_loop(0, count, body, 0, unroll=True)

    place(c0, slab, 0, 8)
    place(c_u, (slab + 3) % NY, 0, 8)
    place(c_d, (slab + 1) % NY, 0, 8)
    place(c_u2, (slab + 2) % NY, 0, 4)
    place(c_d2, (slab + 2) % NY, 4, 4)


def rebuild(pos, occ_index, *pieces):
    return pl.pallas_call(
        rebuild_kernel,
        out_shape=jax.ShapeDtypeStruct((TILES, OCC * HALF, TS), BF),
        in_specs=[SMEM] * 2 + [VMEM] * len(pieces),
        out_specs=VMEM,
        compiler_params=pltpu.CompilerParams(vmem_limit_bytes=16 * 2**20),
        cost_estimate=pl.CostEstimate(flops=0, bytes_accessed=6 * 2**20, transcendentals=0),
        name="rebuild",
    )(pos, occ_index, *pieces)


def main_kernel(pos, pair_tiles, pair_live, dense,
                own0, own_r, own_l, own_r2, own_l2, oth0, oth_r, oth_l, oth_r2, oth_l2,
                keep, send, field, block):
    core, x = pos[1], pos[3]

    def transform(xp, own, oth, lo, count):
        def body(step, carry):
            tile = (lo + step) * NX + xp
            lhs, rhs = [], []
            for part, ref in ((core, own), (1 - core, oth)):
                for j in range(2):
                    slot = part * 2 + j
                    eri = ref[step, j]
                    rhs.append(jnp.where(pair_live[slot, tile] != 0, eri, jnp.zeros_like(eri)))
                    lhs.append(dense[pair_tiles[slot, tile]])
            half = jnp.dot(
                jnp.concatenate(lhs, axis=1), jnp.concatenate(rhs, axis=0), preferred_element_type=F32
            )
            field[tile] = half.astype(BF)
            return carry

        lax.fori_loop(0, count, body, 0, unroll=4)

    transform(x, own0, oth0, 0, 8)
    transform((x + 3) % NX, own_r, oth_r, 0, 8)
    transform((x + 1) % NX, own_l, oth_l, 0, 8)
    transform((x + 2) % NX, own_r2, oth_r2, 0, 4)
    transform((x + 2) % NX, own_l2, oth_l2, 4, 4)

    def gram(zp, carry):
        tile = zp * NX + x
        partners = jnp.concatenate([field[pair_tiles[slot, tile]] for slot in range(SLOTS)], axis=1)
        block[...] = lax.dot_general(
            field[tile], partners, (((0,), (0,)), ((), ())), preferred_element_type=F32
        )
        for y in range(NY):
            near = pl.multiple_of(y * 2 * ROWS + core * ROWS, ROWS)
            far = pl.multiple_of(y * 2 * ROWS + (1 - core) * ROWS, ROWS)
            for slot in range(SLOTS):
                keep[y, zp, slot] = block[pl.ds(near, ROWS), slot * TS:(slot + 1) * TS]
                send[y, zp, slot] = block[pl.ds(far, ROWS), slot * TS:(slot + 1) * TS]
        return carry

    lax.fori_loop(0, NZ, gram, 0)


def exchange(pos, pair_tiles, pair_live, *pieces):
    shape = jax.ShapeDtypeStruct((NY, NZ, SLOTS, ROWS, TS), F32)
    return pl.pallas_call(
        main_kernel,
        out_shape=(shape, shape),
        in_specs=[SMEM] * 3 + [VMEM] * len(pieces),
        out_specs=(VMEM, VMEM),
        scratch_shapes=[
            pltpu.VMEM((TILES, OCC * HALF, TS), BF),
            pltpu.VMEM((TS, SLOTS * TS), F32),
        ],
        compiler_params=pltpu.CompilerParams(vmem_limit_bytes=24 * 2**20),
        cost_estimate=pl.CostEstimate(flops=2700000000, bytes_accessed=10 * 2**20, transcendentals=0),
        name="exchange",
    )(pos, pair_tiles, pair_live, *pieces)


def shift(value, axis, size, by):
    return lax.ppermute(value, axis, [(i, (i + by) % size) for i in range(size)])


def swap(value):
    return lax.ppermute(value, "c", [(0, 1), (1, 0)])


def shards(integrals, orbitals, pair_tiles, pair_live, occ_live):
    pos = jnp.stack([lax.axis_index(name).astype(jnp.int32) for name in ("y", "c", "z", "x")])
    tile = pos[2] * NX + pos[3]
    coeffs = slice_coeffs(pos, occ_live.T, orbitals)
    coeffs, eri = lax.optimization_barrier((coeffs, integrals.reshape(SLOTS * TS * AUXROWS, TS)))
    column = lax.all_to_all(coeffs, "z", split_axis=0, concat_axis=0, tiled=True)
    keep_eri, give_eri = split_aux(pos, eri)
    rank = jnp.cumsum(occ_live, axis=1) - 1
    hits = (occ_live[None] != 0) & (rank[None] == jnp.arange(LIVE)[:, None, None])
    occ_index = jnp.sum(jnp.where(hits, jnp.arange(OCC)[None, None, :], 0), axis=2).astype(jnp.int32)

    got_eri = swap(give_eri)
    c0 = jnp.stack([column] + [shift(column, "x", NX, by) for by in (1, 2, 3)], axis=1)
    got_eri, c0 = lax.optimization_barrier((got_eri, c0))
    by_aux = lax.dynamic_slice_in_dim(
        jnp.concatenate([keep_eri, got_eri, keep_eri]), pos[1] * AUXROWS, NZ, 0
    )
    own0 = lax.all_to_all(by_aux, "z", split_axis=0, concat_axis=0, tiled=True)
    own_r, own_l = shift(own0, "x", NX, 1), shift(own0, "x", NX, -1)
    c_u, c_d = shift(c0, "y", NY, 1), shift(c0, "y", NY, -1)
    oth0 = swap(own0)
    own_r2, own_l2 = shift(own_r[:4], "x", NX, 1), shift(own_l[4:], "x", NX, -1)
    c_u2, c_d2 = shift(c_u[:4], "y", NY, 1), shift(c_d[4:], "y", NY, -1)
    oth_r, oth_l = swap(own_r), swap(own_l)
    oth_r2, oth_l2 = swap(own_r2), swap(own_l2)

    dense = rebuild(pos, occ_index, c0, c_u, c_d, c_u2, c_d2)
    keep, send = exchange(
        pos, pair_tiles.T, pair_live.T, dense,
        own0, own_r, own_l, own_r2, own_l2, oth0, oth_r, oth_l, oth_r2, oth_l2,
    )
    partial = (keep + swap(send)).astype(BF).reshape(NY * NZ, SLOTS, ROWS, TS)
    parts = lax.all_to_all(partial, ("y", "z"), split_axis=0, concat_axis=0, tiled=True).astype(F32)
    flags = lax.dynamic_index_in_dim(pair_live, tile, 0, keepdims=False).astype(F32) * SCALE
    return (jnp.sum(parts, axis=0) * flags[:, None, None])[None]


def solution(mesh):
    grid = Mesh(mesh.devices.reshape(NY, NC, NZ, NX), ("y", "c", "z", "x"))
    return jax.shard_map(
        shards,
        mesh=grid,
        in_specs=(
            P(("z", "x"), None, None, ("y", "c"), None),
            P(("z", "x"), None),
            P(),
            P(),
            P(),
        ),
        out_specs=P(("z", "x"), None, ("y", "c"), None),
        check_vma=False,
    )
```

```python
import functools
import math

import jax
import jax.numpy as jnp
from jax import lax
from jax.experimental import pallas as pl
from jax.experimental.pallas import tpu as pltpu
from jax.sharding import Mesh, PartitionSpec as P

NY, NC, NZ, NX = 4, 2, 8, 4
TILES, SLOTS, TS = 32, 4, 128
OCC, LIVE = 8, 4
AUXROWS = 4
HALF = TS // 2
ROWS = TS // (NY * NC)
SCALE = 1.0 / math.sqrt(32768.0)
BF = jnp.bfloat16
F32 = jnp.float32
VMEM = pl.BlockSpec(memory_space=pltpu.VMEM)
SMEM = pl.BlockSpec(memory_space=pltpu.SMEM)
ANY = pl.BlockSpec(memory_space=pl.ANY)


def slice_kernel(pos, occ_live, orb, coeffs, cols, sem):
    slab, core, tile = pos[0], pos[1], pos[2] * NX + pos[3]
    load = pltpu.make_async_copy(orb, cols, sem)
    load.start()
    load.wait()
    count = jnp.int32(0)
    for occ in range(OCC):
        live = occ_live[occ, tile] != 0

        @pl.when(live & (count == slab))
        def _():
            flipped = cols[:, occ * TS:(occ + 1) * TS].astype(F32).T.astype(BF)
            mine = jnp.where(core == 0, flipped[:HALF], flipped[HALF:])
            for target in range(NZ):
                coeffs[target] = mine

        count = count + jnp.where(live, 1, 0)


def slice_coeffs(pos, occ_live, orb):
    return pl.pallas_call(
        slice_kernel,
        out_shape=jax.ShapeDtypeStruct((NZ, HALF, TS), BF),
        in_specs=[SMEM, SMEM, ANY],
        out_specs=VMEM,
        scratch_shapes=[pltpu.VMEM(orb.shape, BF), pltpu.SemaphoreType.DMA],
        compiler_params=pltpu.CompilerParams(vmem_limit_bytes=60 * 2**20),
        cost_estimate=pl.CostEstimate(flops=0, bytes_accessed=2 * orb.size, transcendentals=0),
        name="slice_coeffs",
    )(pos, occ_live, orb)


def split_kernel(pos, eri, keep, give):
    core = pos[1]
    row = lax.broadcasted_iota(jnp.int32, (TS, TS), 0)
    col = lax.broadcasted_iota(jnp.int32, (TS, TS), 1)
    block_nu = TS // AUXROWS
    perm = (col == (row % block_nu) * AUXROWS + row // block_nu).astype(BF)
    for out, part in ((give, 1 - core), (keep, core)):
        for j in range(2):
            for quarter in range(AUXROWS):
                start = pl.multiple_of(((part * 2 + j) * AUXROWS + quarter) * TS, TS)
                mixed = jnp.dot(perm, eri[pl.ds(start, TS), :], preferred_element_type=F32).astype(BF)
                for aux in range(AUXROWS):
                    out[aux, j, pl.ds(quarter * block_nu, block_nu), :] = mixed[aux * block_nu:(aux + 1) * block_nu]


def split_aux(pos, eri):
    piece = jax.ShapeDtypeStruct((AUXROWS, 2, TS, TS), BF)
    return pl.pallas_call(
        split_kernel,
        out_shape=(piece, piece),
        in_specs=[SMEM, VMEM],
        out_specs=(VMEM, VMEM),
        compiler_params=pltpu.CompilerParams(vmem_limit_bytes=8 * 2**20),
        cost_estimate=pl.CostEstimate(flops=2 * TS * eri.size, bytes_accessed=4 * eri.size, transcendentals=0),
        name="split_aux",
    )(pos, eri)


def rebuild_kernel(pos, occ_index, c0, c_u, c_d, c_u2, c_d2, dense):
    slab, x = pos[0], pos[3]

    def clear(tile, carry):
        dense[tile] = jnp.zeros(dense.shape[1:], BF)
        return carry

    lax.fori_loop(0, TILES, clear, 0, unroll=4)

    def place(piece, k, lo, count):
        def body(step, carry):
            for entry in range(NX):
                tile = (lo + step) * NX + (x - entry + NX) % NX
                start = pl.multiple_of(occ_index[k, tile] * HALF, HALF)
                dense[tile, pl.ds(start, HALF), :] = piece[step, entry]
            return carry

        lax.fori_loop(0, count, body, 0, unroll=True)

    place(c0, slab, 0, 8)
    place(c_u, (slab + 3) % NY, 0, 8)
    place(c_d, (slab + 1) % NY, 0, 8)
    place(c_u2, (slab + 2) % NY, 0, 4)
    place(c_d2, (slab + 2) % NY, 4, 4)


def rebuild(pos, occ_index, *pieces):
    return pl.pallas_call(
        rebuild_kernel,
        out_shape=jax.ShapeDtypeStruct((TILES, OCC * HALF, TS), BF),
        in_specs=[SMEM] * 2 + [VMEM] * len(pieces),
        out_specs=VMEM,
        compiler_params=pltpu.CompilerParams(vmem_limit_bytes=16 * 2**20),
        cost_estimate=pl.CostEstimate(flops=0, bytes_accessed=6 * 2**20, transcendentals=0),
        name="rebuild",
    )(pos, occ_index, *pieces)


def transform(pos, pair_tiles, pair_live, dense, field, first, xp, own, oth, lo, count):
    core = pos[1]

    def body(step, carry):
        tile = (lo + step) * NX + xp
        lhs, rhs = [], []
        for part, ref in ((core, own), (1 - core, oth)):
            for j in range(2):
                slot = part * 2 + j
                eri = ref[step, j]
                rhs.append(jnp.where(pair_live[slot, tile] != 0, eri, jnp.zeros_like(eri)))
                lhs.append(dense[pair_tiles[slot, tile]])
        half = jnp.dot(jnp.concatenate(lhs, axis=1), jnp.concatenate(rhs, axis=0), preferred_element_type=F32)
        field[first + lo + step] = half.astype(BF)
        return carry

    lax.fori_loop(0, count, body, 0, unroll=4)


def near_kernel(pos, pair_tiles, pair_live, dense, own0, own_r, own_l, oth0, oth_rl, field):
    x = pos[3]
    run = functools.partial(transform, pos, pair_tiles, pair_live, dense, field)
    run(0, x, own0, oth0, 0, NZ)
    run(NZ, (x + 3) % NX, own_r, oth_rl.at[0], 0, NZ)
    run(2 * NZ, (x + 1) % NX, own_l, oth_rl.at[1], 0, NZ)


def near_columns(pos, pair_tiles, pair_live, dense, *pieces):
    return pl.pallas_call(
        near_kernel,
        out_shape=jax.ShapeDtypeStruct((3 * NZ, OCC * HALF, TS), BF),
        in_specs=[SMEM] * 3 + [VMEM] * (1 + len(pieces)),
        out_specs=VMEM,
        compiler_params=pltpu.CompilerParams(vmem_limit_bytes=16 * 2**20),
        cost_estimate=pl.CostEstimate(flops=1600000000, bytes_accessed=10 * 2**20, transcendentals=0),
        name="near_columns",
    )(pos, pair_tiles, pair_live, dense, *pieces)


def far_kernel(pos, pair_tiles, pair_live, dense, near, own_r2, own_l2, oth_r2, oth_l2, keep, send, far, block):
    core, x = pos[1], pos[3]
    run = functools.partial(transform, pos, pair_tiles, pair_live, dense, far)
    run(0, (x + 2) % NX, own_r2, oth_r2, 0, 4)
    run(0, (x + 2) % NX, own_l2, oth_l2, 4, 4)

    def partner(slot, tile):
        other = pair_tiles[slot, tile]
        offset = (other % NX - x + NX) % NX
        row = other // NX
        column = jnp.where(offset == 0, 0, jnp.where(offset == 3, 1, 2))
        return jnp.where(offset == 2, far[row], near[column * NZ + row])

    def gram(zp, carry):
        tile = zp * NX + x
        partners = jnp.concatenate([partner(slot, tile) for slot in range(SLOTS)], axis=1)
        block[...] = lax.dot_general(
            near[zp], partners, (((0,), (0,)), ((), ())), preferred_element_type=F32
        )
        for y in range(NY):
            mine = pl.multiple_of(y * 2 * ROWS + core * ROWS, ROWS)
            other = pl.multiple_of(y * 2 * ROWS + (1 - core) * ROWS, ROWS)
            for slot in range(SLOTS):
                keep[y, zp, slot] = block[pl.ds(mine, ROWS), slot * TS:(slot + 1) * TS]
                send[y, zp, slot] = block[pl.ds(other, ROWS), slot * TS:(slot + 1) * TS]
        return carry

    lax.fori_loop(0, NZ, gram, 0)


def far_column(pos, pair_tiles, pair_live, dense, near, *pieces):
    shape = jax.ShapeDtypeStruct((NY, NZ, SLOTS, ROWS, TS), F32)
    return pl.pallas_call(
        far_kernel,
        out_shape=(shape, shape),
        in_specs=[SMEM] * 3 + [VMEM] * (2 + len(pieces)),
        out_specs=(VMEM, VMEM),
        scratch_shapes=[
            pltpu.VMEM((NZ, OCC * HALF, TS), BF),
            pltpu.VMEM((TS, SLOTS * TS), F32),
        ],
        compiler_params=pltpu.CompilerParams(vmem_limit_bytes=16 * 2**20),
        cost_estimate=pl.CostEstimate(flops=1100000000, bytes_accessed=10 * 2**20, transcendentals=0),
        name="far_column",
    )(pos, pair_tiles, pair_live, dense, near, *pieces)


def shift(value, axis, size, by):
    return lax.ppermute(value, axis, [(i, (i + by) % size) for i in range(size)])


def swap(value):
    return lax.ppermute(value, "c", [(0, 1), (1, 0)])


def shards(integrals, orbitals, pair_tiles, pair_live, occ_live):
    pos = jnp.stack([lax.axis_index(name).astype(jnp.int32) for name in ("y", "c", "z", "x")])
    tile = pos[2] * NX + pos[3]
    coeffs = slice_coeffs(pos, occ_live.T, orbitals)
    coeffs, eri = lax.optimization_barrier((coeffs, integrals.reshape(SLOTS * TS * AUXROWS, TS)))
    column = lax.all_to_all(coeffs, "z", split_axis=0, concat_axis=0, tiled=True)
    keep_eri, give_eri = split_aux(pos, eri)
    rank = jnp.cumsum(occ_live, axis=1) - 1
    hits = (occ_live[None] != 0) & (rank[None] == jnp.arange(LIVE)[:, None, None])
    occ_index = jnp.sum(jnp.where(hits, jnp.arange(OCC)[None, None, :], 0), axis=2).astype(jnp.int32)

    got_eri = swap(give_eri)
    got_eri, column = lax.optimization_barrier((got_eri, column))
    by_aux = lax.dynamic_slice_in_dim(
        jnp.concatenate([keep_eri, got_eri, keep_eri]), pos[1] * AUXROWS, NZ, 0
    )
    own0 = lax.all_to_all(by_aux, "z", split_axis=0, concat_axis=0, tiled=True)
    c0 = jnp.stack([column] + [shift(column, "x", NX, by) for by in (1, 2, 3)], axis=1)
    own0, c0 = lax.optimization_barrier((own0, c0))
    own_r, own_l = shift(own0, "x", NX, 1), shift(own0, "x", NX, -1)
    c_u, c_d = shift(c0, "y", NY, 1), shift(c0, "y", NY, -1)
    oth0 = swap(own0)
    own_r, own_l, c_u, c_d, oth0 = lax.optimization_barrier((own_r, own_l, c_u, c_d, oth0))
    own_r2, own_l2 = shift(own_r[:4], "x", NX, 1), shift(own_l[4:], "x", NX, -1)
    c_u2, c_d2 = shift(c_u[:4], "y", NY, 1), shift(c_d[4:], "y", NY, -1)
    oth_rl = swap(jnp.stack([own_r, own_l]))
    tables = (pos, pair_tiles.T, pair_live.T)
    dense = rebuild(pos, occ_index, c0, c_u, c_d, c_u2, c_d2)
    near = near_columns(*tables, dense, own0, own_r, own_l, oth0, oth_rl)
    near, own_r2, own_l2 = lax.optimization_barrier((near, own_r2, own_l2))
    oth_r2, oth_l2 = swap(own_r2), swap(own_l2)
    keep, send = far_column(*tables, dense, near, own_r2, own_l2, oth_r2, oth_l2)
    partial = (keep + swap(send)).astype(BF).reshape(NY * NZ, SLOTS, ROWS, TS)
    parts = lax.all_to_all(partial, ("y", "z"), split_axis=0, concat_axis=0, tiled=True).astype(F32)
    flags = lax.dynamic_index_in_dim(pair_live, tile, 0, keepdims=False).astype(F32) * SCALE
    return (jnp.sum(parts, axis=0) * flags[:, None, None])[None]


def solution(mesh):
    grid = Mesh(mesh.devices.reshape(NY, NC, NZ, NX), ("y", "c", "z", "x"))
    return jax.shard_map(
        shards,
        mesh=grid,
        in_specs=(
            P(("z", "x"), None, None, ("y", "c"), None),
            P(("z", "x"), None),
            P(),
            P(),
            P(),
        ),
        out_specs=P(("z", "x"), None, ("y", "c"), None),
        check_vma=False,
    )
```

```python
import functools
import math

import jax
import jax.numpy as jnp
from jax import lax
from jax.experimental import pallas as pl
from jax.experimental.pallas import tpu as pltpu
from jax.sharding import Mesh, PartitionSpec as P

NY, NC, NZ, NX = 4, 2, 8, 4
TILES, SLOTS, TS = 32, 4, 128
OCC, LIVE = 8, 4
AUXROWS = 4
HALF = TS // 2
ROWS = TS // (NY * NC)
SCALE = 1.0 / math.sqrt(32768.0)
BF = jnp.bfloat16
F32 = jnp.float32
VMEM = pl.BlockSpec(memory_space=pltpu.VMEM)
SMEM = pl.BlockSpec(memory_space=pltpu.SMEM)
ANY = pl.BlockSpec(memory_space=pl.ANY)


def position():
    return tuple(lax.axis_index(name).astype(jnp.int32) for name in ("y", "c", "z", "x"))


def slice_kernel(occ_live, orb, coeffs, cols, sem):
    slab, core, z, x = position()
    tile = z * NX + x
    chosen = jnp.int32(0)
    count = jnp.int32(0)
    for occ in range(OCC):
        live = occ_live[occ, tile] != 0
        chosen = jnp.where(live & (count == slab), occ, chosen)
        count = count + jnp.where(live, 1, 0)
    span = pl.ds(pl.multiple_of(chosen * TS, TS), TS)
    load = pltpu.make_async_copy(orb.at[:, span], cols, sem)
    load.start()
    load.wait()
    flipped = cols[...].astype(F32).T.astype(BF)
    mine = jnp.where(core == 0, flipped[:HALF], flipped[HALF:])
    for target in range(NZ):
        coeffs[target] = mine


def slice_coeffs(occ_live, orb):
    return pl.pallas_call(
        slice_kernel,
        out_shape=jax.ShapeDtypeStruct((NZ, HALF, TS), BF),
        in_specs=[SMEM, ANY],
        out_specs=VMEM,
        scratch_shapes=[pltpu.VMEM((TS, TS), BF), pltpu.SemaphoreType.DMA],
        compiler_params=pltpu.CompilerParams(vmem_limit_bytes=60 * 2**20),
        cost_estimate=pl.CostEstimate(flops=0, bytes_accessed=2 * orb.size, transcendentals=0),
        name="slice_coeffs",
    )(occ_live, orb)


def split_kernel(eri, keep, give):
    core = position()[1]
    row = lax.broadcasted_iota(jnp.int32, (TS, TS), 0)
    col = lax.broadcasted_iota(jnp.int32, (TS, TS), 1)
    block_nu = TS // AUXROWS
    perm = (col == (row % block_nu) * AUXROWS + row // block_nu).astype(BF)
    for out, part in ((give, 1 - core), (keep, core)):
        for j in range(2):
            for quarter in range(AUXROWS):
                start = pl.multiple_of(((part * 2 + j) * AUXROWS + quarter) * TS, TS)
                mixed = jnp.dot(perm, eri[pl.ds(start, TS), :], preferred_element_type=F32).astype(BF)
                for aux in range(AUXROWS):
                    out[aux, j, pl.ds(quarter * block_nu, block_nu), :] = mixed[aux * block_nu:(aux + 1) * block_nu]


def split_aux(eri):
    piece = jax.ShapeDtypeStruct((AUXROWS, 2, TS, TS), BF)
    return pl.pallas_call(
        split_kernel,
        out_shape=(piece, piece),
        in_specs=[VMEM],
        out_specs=(VMEM, VMEM),
        compiler_params=pltpu.CompilerParams(vmem_limit_bytes=8 * 2**20),
        cost_estimate=pl.CostEstimate(flops=2 * TS * eri.size, bytes_accessed=4 * eri.size, transcendentals=0),
        name="split_aux",
    )(eri)


def rebuild_kernel(occ_index, c0, c_u, c_d, c_u2, c_d2, dense):
    slab, _, _, x = position()

    def clear(tile, carry):
        dense[tile] = jnp.zeros(dense.shape[1:], BF)
        return carry

    lax.fori_loop(0, TILES, clear, 0, unroll=4)

    def place(piece, k, lo, count):
        def body(step, carry):
            for entry in range(NX):
                tile = (lo + step) * NX + (x - entry + NX) % NX
                start = pl.multiple_of(occ_index[k, tile] * HALF, HALF)
                dense[tile, pl.ds(start, HALF), :] = piece[step, entry]
            return carry

        lax.fori_loop(0, count, body, 0, unroll=True)

    place(c0, slab, 0, 8)
    place(c_u, (slab + 3) % NY, 0, 8)
    place(c_d, (slab + 1) % NY, 0, 8)
    place(c_u2, (slab + 2) % NY, 0, 4)
    place(c_d2, (slab + 2) % NY, 4, 4)


def rebuild(occ_index, *pieces):
    return pl.pallas_call(
        rebuild_kernel,
        out_shape=jax.ShapeDtypeStruct((TILES, OCC * HALF, TS), BF),
        in_specs=[SMEM] + [VMEM] * len(pieces),
        out_specs=VMEM,
        compiler_params=pltpu.CompilerParams(vmem_limit_bytes=16 * 2**20),
        cost_estimate=pl.CostEstimate(flops=0, bytes_accessed=6 * 2**20, transcendentals=0),
        name="rebuild",
    )(occ_index, *pieces)


def main_kernel(pair_tiles, pair_live, dense,
                own0, own_r, own_l, own_r2, own_l2, oth0, oth_r, oth_l, oth_r2, oth_l2,
                keep, send, field, block):
    _, core, _, x = position()

    def transform(xp, own, oth, lo, count):
        def body(step, carry):
            tile = (lo + step) * NX + xp
            lhs, rhs = [], []
            for part, ref in ((core, own), (1 - core, oth)):
                for j in range(2):
                    slot = part * 2 + j
                    eri = ref[step, j]
                    rhs.append(jnp.where(pair_live[slot, tile] != 0, eri, jnp.zeros_like(eri)))
                    lhs.append(dense[pair_tiles[slot, tile]])
            half = jnp.dot(
                jnp.concatenate(lhs, axis=1), jnp.concatenate(rhs, axis=0), preferred_element_type=F32
            )
            field[tile] = half.astype(BF)
            return carry

        lax.fori_loop(0, count, body, 0, unroll=True)

    transform(x, own0, oth0, 0, 8)
    transform((x + 3) % NX, own_r, oth_r, 0, 8)
    transform((x + 1) % NX, own_l, oth_l, 0, 8)
    transform((x + 2) % NX, own_r2, oth_r2, 0, 4)
    transform((x + 2) % NX, own_l2, oth_l2, 4, 4)

    def gram(zp, carry):
        tile = zp * NX + x
        partners = jnp.concatenate([field[pair_tiles[slot, tile]] for slot in range(SLOTS)], axis=1)
        block[...] = lax.dot_general(
            field[tile], partners, (((0,), (0,)), ((), ())), preferred_element_type=F32
        )
        for y in range(NY):
            near = pl.multiple_of(y * 2 * ROWS + core * ROWS, ROWS)
            far = pl.multiple_of(y * 2 * ROWS + (1 - core) * ROWS, ROWS)
            for slot in range(SLOTS):
                keep[y, zp, slot] = block[pl.ds(near, ROWS), slot * TS:(slot + 1) * TS]
                send[y, zp, slot] = block[pl.ds(far, ROWS), slot * TS:(slot + 1) * TS]
        return carry

    lax.fori_loop(0, NZ, gram, 0)


def exchange(pair_tiles, pair_live, *pieces):
    shape = jax.ShapeDtypeStruct((NY, NZ, SLOTS, ROWS, TS), F32)
    return pl.pallas_call(
        main_kernel,
        out_shape=(shape, shape),
        in_specs=[SMEM] * 2 + [VMEM] * len(pieces),
        out_specs=(VMEM, VMEM),
        scratch_shapes=[
            pltpu.VMEM((TILES, OCC * HALF, TS), BF),
            pltpu.VMEM((TS, SLOTS * TS), F32),
        ],
        compiler_params=pltpu.CompilerParams(vmem_limit_bytes=24 * 2**20),
        cost_estimate=pl.CostEstimate(flops=2700000000, bytes_accessed=10 * 2**20, transcendentals=0),
        name="exchange",
    )(pair_tiles, pair_live, *pieces)


def shift(value, axis, size, by):
    return lax.ppermute(value, axis, [(i, (i + by) % size) for i in range(size)])


def swap(value):
    return lax.ppermute(value, "c", [(0, 1), (1, 0)])


def shards(integrals, orbitals, pair_tiles, pair_live, occ_live):
    _, core, z, x = position()
    tile = z * NX + x
    coeffs = slice_coeffs(occ_live.T, orbitals)
    eri = integrals.reshape(SLOTS * TS * AUXROWS, TS)
    column = lax.all_to_all(coeffs, "z", split_axis=0, concat_axis=0, tiled=True)
    keep_eri, give_eri = split_aux(eri)
    rank = jnp.cumsum(occ_live, axis=1) - 1
    hits = (occ_live[None] != 0) & (rank[None] == jnp.arange(LIVE)[:, None, None])
    occ_index = jnp.sum(jnp.where(hits, jnp.arange(OCC)[None, None, :], 0), axis=2).astype(jnp.int32)

    got_eri = swap(give_eri)
    by_aux = lax.dynamic_slice_in_dim(
        jnp.concatenate([keep_eri, got_eri, keep_eri]), core * AUXROWS, NZ, 0
    )
    by_aux, column = lax.optimization_barrier((by_aux, column))
    own0 = lax.all_to_all(by_aux, "z", split_axis=0, concat_axis=0, tiled=True)
    c0 = jnp.stack([column] + [shift(column, "x", NX, by) for by in (1, 2, 3)], axis=1)
    own_r, own_l = shift(own0, "x", NX, 1), shift(own0, "x", NX, -1)
    c_u, c_d = shift(c0, "y", NY, 1), shift(c0, "y", NY, -1)
    oth0 = swap(own0)
    own_r2, own_l2 = shift(own_r[:4], "x", NX, 1), shift(own_l[4:], "x", NX, -1)
    c_u2, c_d2 = shift(c_u[:4], "y", NY, 1), shift(c_d[4:], "y", NY, -1)
    oth_r, oth_l = swap(own_r), swap(own_l)
    oth_r2, oth_l2 = swap(own_r2), swap(own_l2)

    dense = rebuild(occ_index, c0, c_u, c_d, c_u2, c_d2)
    keep, send = exchange(
        pair_tiles.T, pair_live.T, dense,
        own0, own_r, own_l, own_r2, own_l2, oth0, oth_r, oth_l, oth_r2, oth_l2,
    )
    partial = (keep + swap(send)).astype(BF).reshape(NY * NZ, SLOTS, ROWS, TS)
    parts = lax.all_to_all(partial, ("y", "z"), split_axis=0, concat_axis=0, tiled=True).astype(F32)
    flags = lax.dynamic_index_in_dim(pair_live, tile, 0, keepdims=False).astype(F32) * SCALE
    return (jnp.sum(parts, axis=0) * flags[:, None, None])[None]


def solution(mesh):
    grid = Mesh(mesh.devices.reshape(NY, NC, NZ, NX), ("y", "c", "z", "x"))
    return jax.shard_map(
        shards,
        mesh=grid,
        in_specs=(
            P(("z", "x"), None, None, ("y", "c"), None),
            P(("z", "x"), None),
            P(),
            P(),
            P(),
        ),
        out_specs=P(("z", "x"), None, ("y", "c"), None),
        check_vma=False,
    )
```

```python
import functools
import math

import jax
import jax.numpy as jnp
from jax import lax
from jax.experimental import pallas as pl
from jax.experimental.pallas import tpu as pltpu
from jax.sharding import Mesh, PartitionSpec as P

NY, NC, NZ, NX = 4, 2, 8, 4
TILES, SLOTS, TS = 32, 4, 128
OCC, LIVE = 8, 4
AUXROWS = 4
HALF = TS // 2
ROWS = TS // (NY * NC)
SCALE = 1.0 / math.sqrt(32768.0)
BF = jnp.bfloat16
F32 = jnp.float32
VMEM = pl.BlockSpec(memory_space=pltpu.VMEM)
SMEM = pl.BlockSpec(memory_space=pltpu.SMEM)
ANY = pl.BlockSpec(memory_space=pl.ANY)


def position():
    return tuple(lax.axis_index(name).astype(jnp.int32) for name in ("y", "c", "z", "x"))


def slice_kernel(occ_live, orb, coeffs, cols, sem):
    slab, core, z, x = position()
    tile = z * NX + x
    chosen = jnp.int32(0)
    count = jnp.int32(0)
    for occ in range(OCC):
        live = occ_live[occ, tile] != 0
        chosen = jnp.where(live & (count == slab), occ, chosen)
        count = count + jnp.where(live, 1, 0)
    span = pl.ds(pl.multiple_of(chosen * TS, TS), TS)
    load = pltpu.make_async_copy(orb.at[:, span], cols, sem)
    load.start()
    load.wait()
    flipped = cols[...].astype(F32).T.astype(BF)
    mine = jnp.where(core == 0, flipped[:HALF], flipped[HALF:])
    for target in range(NZ):
        coeffs[target] = mine


def slice_coeffs(occ_live, orb):
    return pl.pallas_call(
        slice_kernel,
        out_shape=jax.ShapeDtypeStruct((NZ, HALF, TS), BF),
        in_specs=[SMEM, ANY],
        out_specs=VMEM,
        scratch_shapes=[pltpu.VMEM((TS, TS), BF), pltpu.SemaphoreType.DMA],
        compiler_params=pltpu.CompilerParams(vmem_limit_bytes=60 * 2**20),
        cost_estimate=pl.CostEstimate(flops=0, bytes_accessed=2 * orb.size, transcendentals=0),
        name="slice_coeffs",
    )(occ_live, orb)


def split_kernel(eri, keep, give):
    core = position()[1]
    row = lax.broadcasted_iota(jnp.int32, (TS, TS), 0)
    col = lax.broadcasted_iota(jnp.int32, (TS, TS), 1)
    block_nu = TS // AUXROWS
    perm = (col == (row % block_nu) * AUXROWS + row // block_nu).astype(BF)
    for out, part in ((give, 1 - core), (keep, core)):
        for j in range(2):
            for quarter in range(AUXROWS):
                start = pl.multiple_of(((part * 2 + j) * AUXROWS + quarter) * TS, TS)
                mixed = jnp.dot(perm, eri[pl.ds(start, TS), :], preferred_element_type=F32).astype(BF)
                for aux in range(AUXROWS):
                    out[aux, j, pl.ds(quarter * block_nu, block_nu), :] = mixed[aux * block_nu:(aux + 1) * block_nu]


def split_aux(eri):
    piece = jax.ShapeDtypeStruct((AUXROWS, 2, TS, TS), BF)
    return pl.pallas_call(
        split_kernel,
        out_shape=(piece, piece),
        in_specs=[VMEM],
        out_specs=(VMEM, VMEM),
        compiler_params=pltpu.CompilerParams(vmem_limit_bytes=8 * 2**20),
        cost_estimate=pl.CostEstimate(flops=2 * TS * eri.size, bytes_accessed=4 * eri.size, transcendentals=0),
        name="split_aux",
    )(eri)


def rebuild_kernel(occ_index, c0, c_u, c_d, c_u2, c_d2, dense):
    slab, _, _, x = position()

    def clear(tile, carry):
        dense[tile] = jnp.zeros(dense.shape[1:], BF)
        return carry

    lax.fori_loop(0, TILES, clear, 0, unroll=4)

    def place(piece, k, lo, count):
        def body(step, carry):
            for entry in range(NX):
                tile = (lo + step) * NX + (x - entry + NX) % NX
                start = pl.multiple_of(occ_index[k, tile] * HALF, HALF)
                dense[tile, pl.ds(start, HALF), :] = piece[step, entry]
            return carry

        lax.fori_loop(0, count, body, 0, unroll=True)

    place(c0, slab, 0, 8)
    place(c_u, (slab + 3) % NY, 0, 8)
    place(c_d, (slab + 1) % NY, 0, 8)
    place(c_u2, (slab + 2) % NY, 0, 4)
    place(c_d2, (slab + 2) % NY, 4, 4)


def rebuild(occ_index, *pieces):
    return pl.pallas_call(
        rebuild_kernel,
        out_shape=jax.ShapeDtypeStruct((TILES, OCC * HALF, TS), BF),
        in_specs=[SMEM] + [VMEM] * len(pieces),
        out_specs=VMEM,
        compiler_params=pltpu.CompilerParams(vmem_limit_bytes=16 * 2**20),
        cost_estimate=pl.CostEstimate(flops=0, bytes_accessed=6 * 2**20, transcendentals=0),
        name="rebuild",
    )(occ_index, *pieces)


def main_kernel(pair_tiles, pair_live, dense,
                own0, own_r, own_l, own_r2, own_l2, oth0, oth_r, oth_l, oth_r2, oth_l2,
                keep, send, field, block):
    _, core, _, x = position()

    def transform(xp, own, oth, lo, count):
        def body(step, carry):
            tile = (lo + step) * NX + xp
            lhs, rhs = [], []
            for part, ref in ((core, own), (1 - core, oth)):
                for j in range(2):
                    slot = part * 2 + j
                    eri = ref[step, j]
                    rhs.append(jnp.where(pair_live[slot, tile] != 0, eri, jnp.zeros_like(eri)))
                    lhs.append(dense[pair_tiles[slot, tile]])
            half = jnp.dot(
                jnp.concatenate(lhs, axis=1), jnp.concatenate(rhs, axis=0), preferred_element_type=F32
            )
            field[tile] = half.astype(BF)
            return carry

        lax.fori_loop(0, count, body, 0, unroll=True)

    transform(x, own0, oth0, 0, 8)
    transform((x + 3) % NX, own_r, oth_r, 0, 8)
    transform((x + 1) % NX, own_l, oth_l, 0, 8)
    transform((x + 2) % NX, own_r2, oth_r2, 0, 4)
    transform((x + 2) % NX, own_l2, oth_l2, 4, 4)

    def gram(zp, carry):
        tile = zp * NX + x
        partners = jnp.concatenate([field[pair_tiles[slot, tile]] for slot in range(SLOTS)], axis=1)
        block[...] = lax.dot_general(
            field[tile], partners, (((0,), (0,)), ((), ())), preferred_element_type=F32
        )
        for y in range(NY):
            near = pl.multiple_of(y * 2 * ROWS + core * ROWS, ROWS)
            far = pl.multiple_of(y * 2 * ROWS + (1 - core) * ROWS, ROWS)
            for slot in range(SLOTS):
                keep[y, zp, slot] = block[pl.ds(near, ROWS), slot * TS:(slot + 1) * TS]
                send[y, zp, slot] = block[pl.ds(far, ROWS), slot * TS:(slot + 1) * TS]
        return carry

    lax.fori_loop(0, NZ, gram, 0, unroll=True)


def exchange(pair_tiles, pair_live, *pieces):
    shape = jax.ShapeDtypeStruct((NY, NZ, SLOTS, ROWS, TS), F32)
    return pl.pallas_call(
        main_kernel,
        out_shape=(shape, shape),
        in_specs=[SMEM] * 2 + [VMEM] * len(pieces),
        out_specs=(VMEM, VMEM),
        scratch_shapes=[
            pltpu.VMEM((TILES, OCC * HALF, TS), BF),
            pltpu.VMEM((TS, SLOTS * TS), F32),
        ],
        compiler_params=pltpu.CompilerParams(vmem_limit_bytes=24 * 2**20),
        cost_estimate=pl.CostEstimate(flops=2700000000, bytes_accessed=10 * 2**20, transcendentals=0),
        name="exchange",
    )(pair_tiles, pair_live, *pieces)


def shift(value, axis, size, by):
    return lax.ppermute(value, axis, [(i, (i + by) % size) for i in range(size)])


def swap(value):
    return lax.ppermute(value, "c", [(0, 1), (1, 0)])


def shards(integrals, orbitals, pair_tiles, pair_live, occ_live):
    _, core, z, x = position()
    tile = z * NX + x
    coeffs = slice_coeffs(occ_live.T, orbitals)
    coeffs, eri = lax.optimization_barrier((coeffs, integrals.reshape(SLOTS * TS * AUXROWS, TS)))
    column = lax.all_to_all(coeffs, "z", split_axis=0, concat_axis=0, tiled=True)
    keep_eri, give_eri = split_aux(eri)
    rank = jnp.cumsum(occ_live, axis=1) - 1
    hits = (occ_live[None] != 0) & (rank[None] == jnp.arange(LIVE)[:, None, None])
    occ_index = jnp.sum(jnp.where(hits, jnp.arange(OCC)[None, None, :], 0), axis=2).astype(jnp.int32)

    got_eri = swap(give_eri)
    by_aux = lax.dynamic_slice_in_dim(
        jnp.concatenate([keep_eri, got_eri, keep_eri]), core * AUXROWS, NZ, 0
    )
    by_aux, column, occ_index = lax.optimization_barrier((by_aux, column, occ_index))
    own0 = lax.all_to_all(by_aux, "z", split_axis=0, concat_axis=0, tiled=True)
    c0 = jnp.stack([column] + [shift(column, "x", NX, by) for by in (1, 2, 3)], axis=1)
    own_r, own_l = shift(own0, "x", NX, 1), shift(own0, "x", NX, -1)
    c_u, c_d = shift(c0, "y", NY, 1), shift(c0, "y", NY, -1)
    oth0 = swap(own0)
    own_r2, own_l2 = shift(own_r[:4], "x", NX, 1), shift(own_l[4:], "x", NX, -1)
    c_u2, c_d2 = shift(c_u[:4], "y", NY, 1), shift(c_d[4:], "y", NY, -1)
    oth_r, oth_l = swap(own_r), swap(own_l)
    oth_r2, oth_l2 = swap(own_r2), swap(own_l2)

    dense = rebuild(occ_index, c0, c_u, c_d, c_u2, c_d2)
    keep, send = exchange(
        pair_tiles.T, pair_live.T, dense,
        own0, own_r, own_l, own_r2, own_l2, oth0, oth_r, oth_l, oth_r2, oth_l2,
    )
    partial = (keep + swap(send)).astype(BF).reshape(NY * NZ, SLOTS, ROWS, TS)
    parts = lax.all_to_all(partial, ("y", "z"), split_axis=0, concat_axis=0, tiled=True).astype(F32)
    flags = lax.dynamic_index_in_dim(pair_live, tile, 0, keepdims=False).astype(F32) * SCALE
    return (jnp.sum(parts, axis=0) * flags[:, None, None])[None]


def solution(mesh):
    grid = Mesh(mesh.devices.reshape(NY, NC, NZ, NX), ("y", "c", "z", "x"))
    return jax.shard_map(
        shards,
        mesh=grid,
        in_specs=(
            P(("z", "x"), None, None, ("y", "c"), None),
            P(("z", "x"), None),
            P(),
            P(),
            P(),
        ),
        out_specs=P(("z", "x"), None, ("y", "c"), None),
        check_vma=False,
    )
```

```python
import functools
import math

import jax
import jax.numpy as jnp
from jax import lax
from jax.experimental import pallas as pl
from jax.experimental.pallas import tpu as pltpu
from jax.sharding import Mesh, PartitionSpec as P

NY, NC, NZ, NX = 4, 2, 8, 4
TILES, SLOTS, TS = 32, 4, 128
OCC, LIVE = 8, 4
AUXROWS = 4
HALF = TS // 2
ROWS = TS // (NY * NC)
SCALE = 1.0 / math.sqrt(32768.0)
BF = jnp.bfloat16
F32 = jnp.float32
VMEM = pl.BlockSpec(memory_space=pltpu.VMEM)
SMEM = pl.BlockSpec(memory_space=pltpu.SMEM)
ANY = pl.BlockSpec(memory_space=pl.ANY)


def position():
    return tuple(lax.axis_index(name).astype(jnp.int32) for name in ("y", "c", "z", "x"))


def prep_kernel(occ_live, orb, eri, coeffs, keep, give, cols, rows, sems):
    slab, core, z, x = position()
    tile = z * NX + x
    size = 2 * AUXROWS * TS
    loads = []
    for index, part in enumerate((1 - core, core)):
        span = pl.ds(pl.multiple_of(part * size, size), size)
        loads.append(pltpu.make_async_copy(eri.at[span], rows.at[span], sems.at[index + 1]))
    chosen = jnp.int32(0)
    count = jnp.int32(0)
    for occ in range(OCC):
        live = occ_live[occ, tile] != 0
        chosen = jnp.where(live & (count == slab), occ, chosen)
        count = count + jnp.where(live, 1, 0)
    span = pl.ds(pl.multiple_of(chosen * TS, TS), TS)
    load = pltpu.make_async_copy(orb.at[:, span], cols, sems.at[0])
    load.start()
    for part in loads:
        part.start()
    load.wait()
    flipped = cols[...].astype(F32).T.astype(BF)
    mine = jnp.where(core == 0, flipped[:HALF], flipped[HALF:])
    for target in range(NZ):
        coeffs[target] = mine
    row = lax.broadcasted_iota(jnp.int32, (TS, TS), 0)
    col = lax.broadcasted_iota(jnp.int32, (TS, TS), 1)
    block_nu = TS // AUXROWS
    perm = (col == (row % block_nu) * AUXROWS + row // block_nu).astype(BF)
    for out, part, load in ((give, 1 - core, loads[0]), (keep, core, loads[1])):
        load.wait()
        for j in range(2):
            for quarter in range(AUXROWS):
                start = pl.multiple_of(((part * 2 + j) * AUXROWS + quarter) * TS, TS)
                mixed = jnp.dot(perm, rows[pl.ds(start, TS), :], preferred_element_type=F32).astype(BF)
                for aux in range(AUXROWS):
                    out[aux, j, pl.ds(quarter * block_nu, block_nu), :] = mixed[aux * block_nu:(aux + 1) * block_nu]


def prep(occ_live, orb, eri):
    piece = jax.ShapeDtypeStruct((AUXROWS, 2, TS, TS), BF)
    return pl.pallas_call(
        prep_kernel,
        out_shape=(jax.ShapeDtypeStruct((NZ, HALF, TS), BF), piece, piece),
        in_specs=[SMEM, ANY, ANY],
        out_specs=(VMEM, VMEM, VMEM),
        scratch_shapes=[pltpu.VMEM((TS, TS), BF), pltpu.VMEM(eri.shape, BF), pltpu.SemaphoreType.DMA((3,))],
        compiler_params=pltpu.CompilerParams(vmem_limit_bytes=60 * 2**20),
        name="prep",
    )(occ_live, orb, eri)


def rebuild_kernel(occ_index, c0, c_u, c_d, c_u2, c_d2, dense):
    slab, _, _, x = position()

    def clear(tile, carry):
        dense[tile] = jnp.zeros(dense.shape[1:], BF)
        return carry

    lax.fori_loop(0, TILES, clear, 0, unroll=4)

    def place(piece, k, lo, count):
        def body(step, carry):
            for entry in range(NX):
                tile = (lo + step) * NX + (x - entry + NX) % NX
                start = pl.multiple_of(occ_index[k, tile] * HALF, HALF)
                dense[tile, pl.ds(start, HALF), :] = piece[step, entry]
            return carry

        lax.fori_loop(0, count, body, 0, unroll=True)

    place(c0, slab, 0, 8)
    place(c_u, (slab + 3) % NY, 0, 8)
    place(c_d, (slab + 1) % NY, 0, 8)
    place(c_u2, (slab + 2) % NY, 0, 4)
    place(c_d2, (slab + 2) % NY, 4, 4)


def rebuild(occ_index, *pieces):
    return pl.pallas_call(
        rebuild_kernel,
        out_shape=jax.ShapeDtypeStruct((TILES, OCC * HALF, TS), BF),
        in_specs=[SMEM] + [VMEM] * len(pieces),
        out_specs=VMEM,
        compiler_params=pltpu.CompilerParams(vmem_limit_bytes=16 * 2**20),
        cost_estimate=pl.CostEstimate(flops=0, bytes_accessed=6 * 2**20, transcendentals=0),
        name="rebuild",
    )(occ_index, *pieces)


def transform(pair_tiles, pair_live, dense, core, own, oth, first, row, xp, count):
    def body(step, carry):
        tile = (row + step) * NX + xp
        lhs, rhs = [], []
        for part, ref in ((core, own), (1 - core, oth)):
            for j in range(2):
                slot = part * 2 + j
                eri = ref[step, j]
                rhs.append(jnp.where(pair_live[slot, tile] != 0, eri, jnp.zeros_like(eri)))
                lhs.append(dense[pair_tiles[slot, tile]])
        half = jnp.dot(jnp.concatenate(lhs, axis=1), jnp.concatenate(rhs, axis=0), preferred_element_type=F32)
        first(step, tile)[...] = half.astype(BF)
        return carry

    lax.fori_loop(0, count, body, 0, unroll=True)


def own_kernel(pair_tiles, pair_live, dense, own0, oth0, column):
    _, core, _, x = position()
    transform(pair_tiles, pair_live, dense, core, own0, oth0, lambda step, tile: column.at[step], 0, x, NZ)


def own_column(pair_tiles, pair_live, *pieces):
    return pl.pallas_call(
        own_kernel,
        out_shape=jax.ShapeDtypeStruct((NZ, OCC * HALF, TS), BF),
        in_specs=[SMEM] * 2 + [VMEM] * len(pieces),
        out_specs=VMEM,
        compiler_params=pltpu.CompilerParams(vmem_limit_bytes=16 * 2**20),
        cost_estimate=pl.CostEstimate(flops=0, bytes_accessed=0, transcendentals=0),
        name="own_column",
    )(pair_tiles, pair_live, *pieces)


def main_kernel(pair_tiles, pair_live, dense,
                column, own_r, own_l, own_r2, own_l2, oth_r, oth_l, oth_r2, oth_l2,
                keep, send, field, block):
    _, core, _, x = position()

    for row in range(NZ):
        field[row * NX + x] = column[row]

    def run(own, oth, row, xp, count):
        transform(pair_tiles, pair_live, dense, core, own, oth, lambda step, tile: field.at[tile], row, xp, count)

    run(own_r, oth_r, 0, (x + 3) % NX, NZ)
    run(own_l, oth_l, 0, (x + 1) % NX, NZ)
    run(own_r2, oth_r2, 0, (x + 2) % NX, 4)
    run(own_l2, oth_l2, 4, (x + 2) % NX, 4)

    def gram(zp, carry):
        tile = zp * NX + x
        partners = jnp.concatenate([field[pair_tiles[slot, tile]] for slot in range(SLOTS)], axis=1)
        block[...] = lax.dot_general(
            field[tile], partners, (((0,), (0,)), ((), ())), preferred_element_type=F32
        )
        for y in range(NY):
            near = pl.multiple_of(y * 2 * ROWS + core * ROWS, ROWS)
            far = pl.multiple_of(y * 2 * ROWS + (1 - core) * ROWS, ROWS)
            for slot in range(SLOTS):
                keep[y, zp, slot] = block[pl.ds(near, ROWS), slot * TS:(slot + 1) * TS]
                send[y, zp, slot] = block[pl.ds(far, ROWS), slot * TS:(slot + 1) * TS]
        return carry

    lax.fori_loop(0, NZ, gram, 0, unroll=True)


def exchange(pair_tiles, pair_live, *pieces):
    shape = jax.ShapeDtypeStruct((NY, NZ, SLOTS, ROWS, TS), F32)
    return pl.pallas_call(
        main_kernel,
        out_shape=(shape, shape),
        in_specs=[SMEM] * 2 + [VMEM] * len(pieces),
        out_specs=(VMEM, VMEM),
        scratch_shapes=[
            pltpu.VMEM((TILES, OCC * HALF, TS), BF),
            pltpu.VMEM((TS, SLOTS * TS), F32),
        ],
        compiler_params=pltpu.CompilerParams(vmem_limit_bytes=24 * 2**20),
        cost_estimate=pl.CostEstimate(flops=2700000000, bytes_accessed=10 * 2**20, transcendentals=0),
        name="exchange",
    )(pair_tiles, pair_live, *pieces)


def shift(value, axis, size, by):
    return lax.ppermute(value, axis, [(i, (i + by) % size) for i in range(size)])


def swap(value):
    return lax.ppermute(value, "c", [(0, 1), (1, 0)])


def shards(integrals, orbitals, pair_tiles, pair_live, occ_live):
    _, core, z, x = position()
    tile = z * NX + x
    coeffs, keep_eri, give_eri = prep(occ_live.T, orbitals, integrals.reshape(SLOTS * TS * AUXROWS, TS))
    column = lax.all_to_all(coeffs, "z", split_axis=0, concat_axis=0, tiled=True)
    rank = jnp.cumsum(occ_live, axis=1) - 1
    hits = (occ_live[None] != 0) & (rank[None] == jnp.arange(LIVE)[:, None, None])
    occ_index = jnp.sum(jnp.where(hits, jnp.arange(OCC)[None, None, :], 0), axis=2).astype(jnp.int32)

    got_eri = swap(give_eri)
    by_aux = lax.dynamic_slice_in_dim(
        jnp.concatenate([keep_eri, got_eri, keep_eri]), core * AUXROWS, NZ, 0
    )
    by_aux, column, occ_index = lax.optimization_barrier((by_aux, column, occ_index))
    own0 = lax.all_to_all(by_aux, "z", split_axis=0, concat_axis=0, tiled=True)
    c0 = jnp.stack([column] + [shift(column, "x", NX, by) for by in (1, 2, 3)], axis=1)
    own_r, own_l = shift(own0, "x", NX, 1), shift(own0, "x", NX, -1)
    c_u, c_d = shift(c0, "y", NY, 1), shift(c0, "y", NY, -1)
    oth0 = swap(own0)
    own_r2, own_l2 = shift(own_r[:4], "x", NX, 1), shift(own_l[4:], "x", NX, -1)
    c_u2, c_d2 = shift(c_u[:4], "y", NY, 1), shift(c_d[4:], "y", NY, -1)
    oth_r, oth_l = swap(own_r), swap(own_l)
    dense = rebuild(occ_index, c0, c_u, c_d, c_u2, c_d2)
    column = own_column(pair_tiles.T, pair_live.T, dense, own0, oth0)
    column, own_r2, own_l2 = lax.optimization_barrier((column, own_r2, own_l2))
    oth_r2, oth_l2 = swap(own_r2), swap(own_l2)

    keep, send = exchange(
        pair_tiles.T, pair_live.T, dense,
        column, own_r, own_l, own_r2, own_l2, oth_r, oth_l, oth_r2, oth_l2,
    )
    partial = (keep + swap(send)).astype(BF).reshape(NY * NZ, SLOTS, ROWS, TS)
    parts = lax.all_to_all(partial, ("y", "z"), split_axis=0, concat_axis=0, tiled=True).astype(F32)
    flags = lax.dynamic_index_in_dim(pair_live, tile, 0, keepdims=False).astype(F32) * SCALE
    return (jnp.sum(parts, axis=0) * flags[:, None, None])[None]


def solution(mesh):
    grid = Mesh(mesh.devices.reshape(NY, NC, NZ, NX), ("y", "c", "z", "x"))
    return jax.shard_map(
        shards,
        mesh=grid,
        in_specs=(
            P(("z", "x"), None, None, ("y", "c"), None),
            P(("z", "x"), None),
            P(),
            P(),
            P(),
        ),
        out_specs=P(("z", "x"), None, ("y", "c"), None),
        check_vma=False,
    )
```

```python
import functools
import math

import jax
import jax.numpy as jnp
from jax import lax
from jax.experimental import pallas as pl
from jax.experimental.pallas import tpu as pltpu
from jax.sharding import Mesh, PartitionSpec as P

NY, NC, NZ, NX = 4, 2, 8, 4
TILES, SLOTS, TS = 32, 4, 128
OCC, LIVE = 8, 4
AUXROWS = 4
HALF = TS // 2
ROWS = TS // (NY * NC)
SCALE = 1.0 / math.sqrt(32768.0)
BF = jnp.bfloat16
F32 = jnp.float32
VMEM = pl.BlockSpec(memory_space=pltpu.VMEM)
SMEM = pl.BlockSpec(memory_space=pltpu.SMEM)
ANY = pl.BlockSpec(memory_space=pl.ANY)


def position():
    return tuple(lax.axis_index(name).astype(jnp.int32) for name in ("y", "c", "z", "x"))


def prep_kernel(occ_live, orb, eri, coeffs, keep, give, cols, rows, sems):
    slab, core, z, x = position()
    tile = z * NX + x
    size = 2 * AUXROWS * TS
    loads = []
    for index, part in enumerate((1 - core, core)):
        span = pl.ds(pl.multiple_of(part * size, size), size)
        loads.append(pltpu.make_async_copy(eri.at[span], rows.at[span], sems.at[index + 1]))
    chosen = jnp.int32(0)
    count = jnp.int32(0)
    for occ in range(OCC):
        live = occ_live[occ, tile] != 0
        chosen = jnp.where(live & (count == slab), occ, chosen)
        count = count + jnp.where(live, 1, 0)
    span = pl.ds(pl.multiple_of(chosen * TS, TS), TS)
    load = pltpu.make_async_copy(orb.at[:, span], cols, sems.at[0])
    load.start()
    for part in loads:
        part.start()
    load.wait()
    flipped = cols[...].astype(F32).T.astype(BF)
    mine = jnp.where(core == 0, flipped[:HALF], flipped[HALF:])
    for target in range(NZ):
        coeffs[target] = mine
    row = lax.broadcasted_iota(jnp.int32, (TS, TS), 0)
    col = lax.broadcasted_iota(jnp.int32, (TS, TS), 1)
    block_nu = TS // AUXROWS
    perm = (col == (row % block_nu) * AUXROWS + row // block_nu).astype(BF)
    for out, part, load in ((give, 1 - core, loads[0]), (keep, core, loads[1])):
        load.wait()
        for j in range(2):
            for quarter in range(AUXROWS):
                start = pl.multiple_of(((part * 2 + j) * AUXROWS + quarter) * TS, TS)
                mixed = jnp.dot(perm, rows[pl.ds(start, TS), :], preferred_element_type=F32).astype(BF)
                for aux in range(AUXROWS):
                    out[aux, j, pl.ds(quarter * block_nu, block_nu), :] = mixed[aux * block_nu:(aux + 1) * block_nu]


def prep(occ_live, orb, eri):
    piece = jax.ShapeDtypeStruct((AUXROWS, 2, TS, TS), BF)
    return pl.pallas_call(
        prep_kernel,
        out_shape=(jax.ShapeDtypeStruct((NZ, HALF, TS), BF), piece, piece),
        in_specs=[SMEM, ANY, ANY],
        out_specs=(VMEM, VMEM, VMEM),
        scratch_shapes=[pltpu.VMEM((TS, TS), BF), pltpu.VMEM(eri.shape, BF), pltpu.SemaphoreType.DMA((3,))],
        compiler_params=pltpu.CompilerParams(vmem_limit_bytes=60 * 2**20),
        name="prep",
    )(occ_live, orb, eri)


def rebuild_kernel(occ_index, c0, c_u, c_d, c_u2, c_d2, dense):
    slab, _, _, x = position()

    def clear(tile, carry):
        dense[tile] = jnp.zeros(dense.shape[1:], BF)
        return carry

    lax.fori_loop(0, TILES, clear, 0, unroll=4)

    def place(piece, k, lo, count):
        def body(step, carry):
            for entry in range(NX):
                tile = (lo + step) * NX + (x - entry + NX) % NX
                start = pl.multiple_of(occ_index[k, tile] * HALF, HALF)
                dense[tile, pl.ds(start, HALF), :] = piece[step, entry]
            return carry

        lax.fori_loop(0, count, body, 0, unroll=True)

    place(c0, slab, 0, 8)
    place(c_u, (slab + 3) % NY, 0, 8)
    place(c_d, (slab + 1) % NY, 0, 8)
    place(c_u2, (slab + 2) % NY, 0, 4)
    place(c_d2, (slab + 2) % NY, 4, 4)


def rebuild(occ_index, *pieces):
    return pl.pallas_call(
        rebuild_kernel,
        out_shape=jax.ShapeDtypeStruct((TILES, OCC * HALF, TS), BF),
        in_specs=[SMEM] + [VMEM] * len(pieces),
        out_specs=VMEM,
        compiler_params=pltpu.CompilerParams(vmem_limit_bytes=16 * 2**20),
        cost_estimate=pl.CostEstimate(flops=0, bytes_accessed=6 * 2**20, transcendentals=0),
        name="rebuild",
    )(occ_index, *pieces)


def transform(pair_tiles, pair_live, dense, core, own, oth, first, row, xp, count):
    def body(step, carry):
        tile = (row + step) * NX + xp
        lhs, rhs = [], []
        for part, ref in ((core, own), (1 - core, oth)):
            for j in range(2):
                slot = part * 2 + j
                eri = ref[step, j]
                rhs.append(jnp.where(pair_live[slot, tile] != 0, eri, jnp.zeros_like(eri)))
                lhs.append(dense[pair_tiles[slot, tile]])
        half = jnp.dot(jnp.concatenate(lhs, axis=1), jnp.concatenate(rhs, axis=0), preferred_element_type=F32)
        first(step, tile)[...] = half.astype(BF)
        return carry

    lax.fori_loop(0, count, body, 0, unroll=True)


def own_kernel(pair_tiles, pair_live, dense, own0, oth0, column):
    _, core, _, x = position()
    transform(pair_tiles, pair_live, dense, core, own0, oth0, lambda step, tile: column.at[step], 0, x, NZ)


def own_column(pair_tiles, pair_live, *pieces):
    return pl.pallas_call(
        own_kernel,
        out_shape=jax.ShapeDtypeStruct((NZ, OCC * HALF, TS), BF),
        in_specs=[SMEM] * 2 + [VMEM] * len(pieces),
        out_specs=VMEM,
        compiler_params=pltpu.CompilerParams(vmem_limit_bytes=16 * 2**20),
        cost_estimate=pl.CostEstimate(flops=0, bytes_accessed=0, transcendentals=0),
        name="own_column",
    )(pair_tiles, pair_live, *pieces)


def main_kernel(pair_tiles, pair_live, dense,
                column, own_r, own_l, own_r2, own_l2, oth_r, oth_l, oth_r2, oth_l2,
                keep, send, field, block):
    _, core, _, x = position()

    for row in range(NZ):
        field[row * NX + x] = column[row]

    def run(own, oth, row, xp, count):
        transform(pair_tiles, pair_live, dense, core, own, oth, lambda step, tile: field.at[tile], row, xp, count)

    run(own_r, oth_r, 0, (x + 3) % NX, NZ)
    run(own_l, oth_l, 0, (x + 1) % NX, NZ)
    run(own_r2, oth_r2, 0, (x + 2) % NX, 4)
    run(own_l2, oth_l2, 4, (x + 2) % NX, 4)

    def gram(zp, carry):
        tile = zp * NX + x
        partners = jnp.concatenate([field[pair_tiles[slot, tile]] for slot in range(SLOTS)], axis=1)
        block[...] = lax.dot_general(
            field[tile], partners, (((0,), (0,)), ((), ())), preferred_element_type=F32
        )
        for y in range(NY):
            near = pl.multiple_of(y * 2 * ROWS + core * ROWS, ROWS)
            far = pl.multiple_of(y * 2 * ROWS + (1 - core) * ROWS, ROWS)
            for slot in range(SLOTS):
                keep[y, zp, slot] = block[pl.ds(near, ROWS), slot * TS:(slot + 1) * TS]
                send[y, zp, slot] = block[pl.ds(far, ROWS), slot * TS:(slot + 1) * TS].astype(BF)
        return carry

    lax.fori_loop(0, NZ, gram, 0, unroll=True)


def exchange(pair_tiles, pair_live, *pieces):
    shape = (NY, NZ, SLOTS, ROWS, TS)
    return pl.pallas_call(
        main_kernel,
        out_shape=(jax.ShapeDtypeStruct(shape, F32), jax.ShapeDtypeStruct(shape, BF)),
        in_specs=[SMEM] * 2 + [VMEM] * len(pieces),
        out_specs=(VMEM, VMEM),
        scratch_shapes=[
            pltpu.VMEM((TILES, OCC * HALF, TS), BF),
            pltpu.VMEM((TS, SLOTS * TS), F32),
        ],
        compiler_params=pltpu.CompilerParams(vmem_limit_bytes=24 * 2**20),
        cost_estimate=pl.CostEstimate(flops=2700000000, bytes_accessed=10 * 2**20, transcendentals=0),
        name="exchange",
    )(pair_tiles, pair_live, *pieces)


def shift(value, axis, size, by):
    return lax.ppermute(value, axis, [(i, (i + by) % size) for i in range(size)])


def swap(value):
    return lax.ppermute(value, "c", [(0, 1), (1, 0)])


def shards(integrals, orbitals, pair_tiles, pair_live, occ_live):
    _, core, z, x = position()
    tile = z * NX + x
    coeffs, keep_eri, give_eri = prep(occ_live.T, orbitals, integrals.reshape(SLOTS * TS * AUXROWS, TS))
    column = lax.all_to_all(coeffs, "z", split_axis=0, concat_axis=0, tiled=True)
    rank = jnp.cumsum(occ_live, axis=1) - 1
    hits = (occ_live[None] != 0) & (rank[None] == jnp.arange(LIVE)[:, None, None])
    occ_index = jnp.sum(jnp.where(hits, jnp.arange(OCC)[None, None, :], 0), axis=2).astype(jnp.int32)

    got_eri = swap(give_eri)
    by_aux = lax.dynamic_slice_in_dim(
        jnp.concatenate([keep_eri, got_eri, keep_eri]), core * AUXROWS, NZ, 0
    )
    by_aux, column, occ_index = lax.optimization_barrier((by_aux, column, occ_index))
    own0 = lax.all_to_all(by_aux, "z", split_axis=0, concat_axis=0, tiled=True)
    c0 = jnp.stack([column] + [shift(column, "x", NX, by) for by in (1, 2, 3)], axis=1)
    own_r, own_l = shift(own0, "x", NX, 1), shift(own0, "x", NX, -1)
    c_u, c_d = shift(c0, "y", NY, 1), shift(c0, "y", NY, -1)
    oth0 = swap(own0)
    own_r2, own_l2 = shift(own_r[:4], "x", NX, 1), shift(own_l[4:], "x", NX, -1)
    c_u2, c_d2 = shift(c_u[:4], "y", NY, 1), shift(c_d[4:], "y", NY, -1)
    oth_r, oth_l = swap(own_r), swap(own_l)
    dense = rebuild(occ_index, c0, c_u, c_d, c_u2, c_d2)
    column = own_column(pair_tiles.T, pair_live.T, dense, own0, oth0)
    column, own_r2, own_l2 = lax.optimization_barrier((column, own_r2, own_l2))
    oth_r2, oth_l2 = swap(own_r2), swap(own_l2)

    keep, send = exchange(
        pair_tiles.T, pair_live.T, dense,
        column, own_r, own_l, own_r2, own_l2, oth_r, oth_l, oth_r2, oth_l2,
    )
    partial = (keep + swap(send).astype(F32)).astype(BF).reshape(NY * NZ, SLOTS, ROWS, TS)
    parts = lax.all_to_all(partial, ("y", "z"), split_axis=0, concat_axis=0, tiled=True).astype(F32)
    flags = lax.dynamic_index_in_dim(pair_live, tile, 0, keepdims=False).astype(F32) * SCALE
    return (jnp.sum(parts, axis=0) * flags[:, None, None])[None]


def solution(mesh):
    grid = Mesh(mesh.devices.reshape(NY, NC, NZ, NX), ("y", "c", "z", "x"))
    return jax.shard_map(
        shards,
        mesh=grid,
        in_specs=(
            P(("z", "x"), None, None, ("y", "c"), None),
            P(("z", "x"), None),
            P(),
            P(),
            P(),
        ),
        out_specs=P(("z", "x"), None, ("y", "c"), None),
        check_vma=False,
    )
```
